32 devices in a mesh: row: 4 (over x, core), col: 8 (over z, y).
Axes of the slice: x: 2, y: 2, z: 4, core: 2. Of those that a mesh axis runs over, the one named last changes fastest.
Arguments:
- first_alignment_matrix: float32 [16, 128, 32], P('row', 'col'), may hold values from -6 to 6
- second_alignment_matrix: float32 [16, 128, 32], P('row', 'col'), may hold values from -6 to 6
- couple_delta_sensitivity: float32 [128, 128, 128], P('row', 'col'), may hold values from -6 to 6
- mapping_matrix: float32 [1024, 128], replicated, may hold values from -0.1875 to 0.1875
Outputs:
- grad_left: float32 [16, 128, 32], P('row', 'col')
- grad_right: float32 [16, 128, 32], P('row', 'col')
The draws below stay inside these ranges and needn't reach their ends.
All inputs are finite; a program needn't handle non-finite values.
Results may differ from the reference program's by a relative error of at most 0.0003.
Values sent between devices are 32-bit elements; how exact they have to be, the bound alone decides.
A program may use at most 64 MiB of HBM per device.

```python
import jax
import jax.numpy as jnp
from jax import lax

FIRST_FEATURES = 32
SECOND_FEATURES = 32
P_SIZE = 128
RES_DEV = 16
ALIGNED_SEQS = 16
AMINO_TOTAL = 128
N_COL = 8


def block_scale(stream_key, dims, shards, smallest, top_value):
    def one(position, shards_of):
        draws = jax.random.uniform(jax.random.fold_in(jax.random.fold_in(stream_key, 6), position), (shards_of,), jnp.float32, smallest / len(shards), top_value / len(shards))
        return jnp.repeat(jnp.exp(draws), dims[position] // shards_of).reshape((-1,) + (1,) * (len(dims) - position - 1))

    gain = one(*shards[0])
    for cut in shards[1:]:
        gain = gain * one(*cut)
    return gain


def noise(stream_key, extent, width, limit, cuts=(), held_as=jnp.bfloat16):
    values = width * jax.random.normal(stream_key, extent, jnp.float32)
    if cuts:
        values = values * block_scale(stream_key, extent, cuts, -0.22, 0.18)
    return jnp.clip(values, -limit, limit).astype(held_as)


def setup_inputs(seed: int = 0) -> dict:
    keys = jax.random.split(jax.random.key(seed), 5)
    return {
        "first_alignment_matrix": noise(keys[0], (ALIGNED_SEQS, AMINO_TOTAL, FIRST_FEATURES), 1.0, 6.0, ((0, 4), (1, 8)), jnp.float32),
        "second_alignment_matrix": noise(keys[1], (ALIGNED_SEQS, AMINO_TOTAL, SECOND_FEATURES), 1.0, 6.0, ((0, 4), (1, 8)), jnp.float32),
        "couple_delta_sensitivity": noise(keys[2], (AMINO_TOTAL, AMINO_TOTAL, P_SIZE), 1.0, 6.0, ((0, 4), (1, 8)), jnp.float32),
        "mapping_matrix": noise(keys[3], (FIRST_FEATURES * SECOND_FEATURES, P_SIZE), (FIRST_FEATURES * SECOND_FEATURES) ** -0.5, 0.1875, (), jnp.float32),
    }


def reference(first_alignment_matrix, second_alignment_matrix, couple_delta_sensitivity, mapping_matrix):
    exact_arithmetic = lax.Precision.HIGHEST
    summed_extent = first_alignment_matrix.shape[0]
    weight3 = mapping_matrix.reshape(FIRST_FEATURES, SECOND_FEATURES, P_SIZE)

    def left_block(index):
        start = (index * RES_DEV).astype(jnp.int32)
        amino_block = lax.dynamic_slice_in_dim(couple_delta_sensitivity, start, RES_DEV, 0)
        dotted_result = jnp.einsum('hiw,gic->hgwc', amino_block, second_alignment_matrix, precision=exact_arithmetic)
        return jnp.einsum('ispe,cep->sic', dotted_result, weight3, precision=exact_arithmetic) / summed_extent

    def right_block(index):
        start = (index * RES_DEV).astype(jnp.int32)
        amino_block = lax.dynamic_slice_in_dim(couple_delta_sensitivity, start, RES_DEV, 1)
        dotted_result = jnp.einsum('gdl,pgv->dplv', amino_block, first_alignment_matrix, precision=exact_arithmetic)
        return jnp.einsum('jspc,cep->sje', dotted_result, weight3, precision=exact_arithmetic) / summed_extent

    steps = jnp.arange(N_COL, dtype=jnp.int32)
    left_parts = lax.map(left_block, steps)
    right_parts = lax.map(right_block, steps)
    grad_left = jnp.transpose(left_parts, (1, 0, 2, 3)).reshape(summed_extent, AMINO_TOTAL, FIRST_FEATURES)
    grad_right = jnp.transpose(right_parts, (1, 0, 2, 3)).reshape(summed_extent, AMINO_TOTAL, SECOND_FEATURES)
    return (grad_left, grad_right)
```

```python
import functools

import jax
import jax.numpy as jnp
from jax import lax
from jax.experimental import pallas as pl
from jax.experimental.pallas import tpu as pltpu
from jax.sharding import PartitionSpec as P

MESH = pl.DeviceIdType.MESH
WIDE = 256
LANES = 128


def split(x):
    high = x.astype(jnp.bfloat16)
    low = (x - high.astype(jnp.float32)).astype(jnp.bfloat16)
    return high, low


def dot_nt(x, y):
    return lax.dot_general(x, y, (((1,), (1,)), ((), ())), preferred_element_type=jnp.float32)


def kernel(
    rows, cols,
    a_ref, b_ref, d_hbm, w_hbm, left_ref, right_ref,
    a_all, b_all, d_buf, w_buf, a_high, a_low, b_high, b_low,
    g_high, g_low, h_high, h_low,
    left_send, right_send, left_recv, right_recv, turned,
    local_sem, a_send_sem, a_recv_sem, b_send_sem, b_recv_sem,
    l_send_sem, l_recv_sem, r_send_sem, r_recv_sem,
):
    seqs, res, feats = a_ref.shape
    feats_e = b_ref.shape[2]
    tile_j = res
    tile_i = d_hbm.shape[0] // tile_j
    halves = tile_i // res
    total = seqs * rows
    group_c = WIDE // feats_e
    group_e = WIDE // feats
    chunks_c = feats // group_c
    chunks_e = feats_e // group_e
    piece_l = seqs * group_c
    piece_r = seqs * group_e

    r = lax.axis_index("row")
    q = lax.axis_index("col")
    owner_row = q // halves
    part = q % halves
    inside = owner_row == r

    copy_d = pltpu.make_async_copy(d_hbm, d_buf, local_sem.at[0])
    copy_w = pltpu.make_async_copy(w_hbm, w_buf, local_sem.at[1])
    copy_d.start()
    copy_w.start()

    barrier = pltpu.get_barrier_semaphore()

    def signal(row, col):
        pl.semaphore_signal(barrier, inc=1, device_id=(row, col), device_id_type=MESH)

    def unless_self(row, col, act, mine=None):
        same = jnp.logical_and(row == r, col == q)
        pl.when(jnp.logical_not(same))(act)
        if mine is not None:
            pl.when(same)(mine)

    for k in range(cols):
        unless_self(owner_row, k, functools.partial(signal, owner_row, k))
    for k in range(rows):
        for h in range(halves):
            col = r * halves + h
            unless_self(k, col, functools.partial(signal, k, col))
    for step in range(1, rows):
        signal((r + step) % rows, q)

    b_all[r] = b_ref[...]

    @pl.when(inside)
    def _():
        a_all[part, r] = a_ref[...]

    pl.semaphore_wait(barrier, (rows - 1) + 2 * jnp.where(inside, cols - 1, cols))

    def copy_b(step):
        dest = (r + step) % rows
        return pltpu.make_async_remote_copy(
            src_ref=b_ref, dst_ref=b_all.at[r], send_sem=b_send_sem.at[step],
            recv_sem=b_recv_sem.at[r], device_id=(dest, q), device_id_type=MESH)

    def copy_a(k):
        return pltpu.make_async_remote_copy(
            src_ref=a_ref, dst_ref=a_all.at[part, r], send_sem=a_send_sem.at[k],
            recv_sem=a_recv_sem.at[part, r], device_id=(owner_row, k), device_id_type=MESH)

    for step in range(1, rows):
        copy_b(step).start()
    for k in range(cols):
        unless_self(owner_row, k, lambda k=k: copy_a(k).start())

    copy_d.wait()
    copy_w.wait()
    d_plain = d_buf[...]
    d_turned = jnp.concatenate(
        [d_buf[pl.ds(j, tile_i, stride=tile_j), :] for j in range(tile_j)], axis=0)

    def expand(d, w, high_ref, low_ref, chunks):
        d_high, d_low = split(d)
        d_both = jnp.concatenate([d_high, d_low], axis=1)
        for n in range(chunks):
            w_high, w_low = split(w[n])
            out = dot_nt(d_both, jnp.concatenate([w_high, w_high], axis=1))
            out = out + dot_nt(d_high, w_low)
            out_high, out_low = split(out)
            high_ref[n] = out_high
            low_ref[n] = out_low

    expand(d_turned, [w_buf[n * WIDE:(n + 1) * WIDE, :] for n in range(chunks_c)],
           g_high, g_low, chunks_c)
    expand(d_plain, [jnp.concatenate(
        [w_buf[pl.ds(n * group_e + e, feats, stride=feats_e), :] for e in range(group_e)], axis=0)
        for n in range(chunks_e)], h_high, h_low, chunks_e)

    def repeat_lanes(x, high_ref, low_ref):
        width = x.shape[1]
        place = lax.broadcasted_iota(jnp.int32, (width, LANES), 1) % width
        unit = (place == lax.broadcasted_iota(jnp.int32, (width, LANES), 0)).astype(jnp.bfloat16)
        high, low = split(x)
        high_ref[...] = jnp.dot(high, unit, preferred_element_type=jnp.float32)
        low_ref[...] = jnp.dot(low, unit, preferred_element_type=jnp.float32)

    def spread(ref, start, stride, group, width):
        x = ref[pl.ds(start, total, stride=stride), :]
        x = jnp.concatenate([x] * (WIDE // LANES), axis=1)
        lane = lax.broadcasted_iota(jnp.int32, (1, group, WIDE), 2) // width
        keep = lane == lax.broadcasted_iota(jnp.int32, (1, group, WIDE), 1)
        x = jnp.where(keep, x[:, None, :], 0.0)
        return x.reshape(total * group, WIDE).astype(jnp.bfloat16)

    def contract(coef_high, coef_low, mat_high, mat_low):
        size = coef_high.shape[0]
        both = dot_nt(jnp.concatenate([coef_high, coef_low], axis=0), mat_high)
        return both[:size] + both[size:] + dot_nt(coef_high, mat_low)

    for step in range(1, rows):
        source = (r + step) % rows
        pltpu.make_async_remote_copy(
            src_ref=b_ref, dst_ref=b_all.at[source], send_sem=b_send_sem.at[step],
            recv_sem=b_recv_sem.at[source], device_id=(source, q), device_id_type=MESH).wait_recv()
    repeat_lanes(b_all[...].reshape(total * tile_j, feats_e), b_high, b_low)
    sum_left = None
    for j in range(tile_j):
        span = slice(j * tile_i, (j + 1) * tile_i)
        term = contract(
            spread(b_high, j, tile_j, group_c, feats_e),
            spread(b_low, j, tile_j, group_c, feats_e),
            jnp.concatenate([g_high[n, span, :] for n in range(chunks_c)], axis=0),
            jnp.concatenate([g_low[n, span, :] for n in range(chunks_c)], axis=0))
        sum_left = term if sum_left is None else sum_left + term
    left_send[...] = sum_left.reshape(rows, piece_l, chunks_c * tile_i)

    def copy_l(k, h):
        return pltpu.make_async_remote_copy(
            src_ref=left_send.at[k], dst_ref=left_recv.at[q], send_sem=l_send_sem.at[k, h],
            recv_sem=l_recv_sem.at[q], device_id=(k, r * halves + h), device_id_type=MESH)

    for k in range(rows):
        for h in range(halves):
            def mine(k=k):
                left_recv[q] = left_send[k]

            unless_self(k, r * halves + h, lambda k=k, h=h: copy_l(k, h).start(), mine)

    for k in range(rows):
        for h in range(halves):
            def arrive(k=k, h=h):
                pltpu.make_async_remote_copy(
                    src_ref=a_ref, dst_ref=a_all.at[h, k], send_sem=a_send_sem.at[0],
                    recv_sem=a_recv_sem.at[h, k], device_id=(k, r * halves + h),
                    device_id_type=MESH).wait_recv()

            unless_self(k, r * halves + h, arrive)
    repeat_lanes(a_all[...].reshape(total * tile_i, feats), a_high, a_low)
    sum_right = None
    for i in range(tile_i):
        span = slice(i * tile_j, (i + 1) * tile_j)
        start = (i // res) * total * res + i % res
        term = contract(
            spread(a_high, start, res, group_e, feats),
            spread(a_low, start, res, group_e, feats),
            jnp.concatenate([h_high[n, span, :] for n in range(chunks_e)], axis=0),
            jnp.concatenate([h_low[n, span, :] for n in range(chunks_e)], axis=0))
        sum_right = term if sum_right is None else sum_right + term
    right_send[...] = sum_right.reshape(rows, piece_r, chunks_e * tile_j)
    right_recv[r] = right_send[r]

    def copy_r(step):
        dest = (r + step) % rows
        return pltpu.make_async_remote_copy(
            src_ref=right_send.at[dest], dst_ref=right_recv.at[r], send_sem=r_send_sem.at[step],
            recv_sem=r_recv_sem.at[r], device_id=(dest, q), device_id_type=MESH)

    for step in range(1, rows):
        copy_r(step).start()

    for k in range(cols):
        def arrive(k=k):
            pltpu.make_async_remote_copy(
                src_ref=left_send.at[0], dst_ref=left_recv.at[k], send_sem=l_send_sem.at[0, 0],
                recv_sem=l_recv_sem.at[k], device_id=(owner_row, k),
                device_id_type=MESH).wait_recv()

        unless_self(owner_row, k, arrive)
    done = jnp.sum(left_recv[...], axis=0) / total
    turned[...] = done.T
    for n in range(chunks_c):
        rows_n = turned[pl.ds(n * tile_i + part * res, res), :]
        for s in range(seqs):
            left_ref[s, :, n * group_c:(n + 1) * group_c] = rows_n[:, s * group_c:(s + 1) * group_c]

    for step in range(1, rows):
        source = (r + step) % rows
        pltpu.make_async_remote_copy(
            src_ref=right_send.at[source], dst_ref=right_recv.at[source],
            send_sem=r_send_sem.at[step], recv_sem=r_recv_sem.at[source],
            device_id=(source, q), device_id_type=MESH).wait_recv()
    done = (jnp.sum(right_recv[...], axis=0) / total).T
    for n in range(chunks_e):
        for s in range(seqs):
            right_ref[s, :, n * group_e:(n + 1) * group_e] = done[
                n * tile_j:(n + 1) * tile_j, s * group_e:(s + 1) * group_e]

    for step in range(1, rows):
        copy_b(step).wait_send()
        copy_r(step).wait_send()
    for k in range(cols):
        unless_self(owner_row, k, lambda k=k: copy_a(k).wait_send())
    for k in range(rows):
        for h in range(halves):
            unless_self(k, r * halves + h, lambda k=k, h=h: copy_l(k, h).wait_send())


def on_device(rows, cols, a, b, d, w):
    seqs, res, feats = a.shape
    feats_e = b.shape[2]
    tile_i, tile_j, pair = d.shape
    halves = tile_i // res
    total = seqs * rows
    group_c, group_e = WIDE // feats_e, WIDE // feats
    chunks_c, chunks_e = feats // group_c, feats_e // group_e
    pairs = tile_i * tile_j
    vmem = pl.BlockSpec(memory_space=pltpu.VMEM)
    anywhere = pl.BlockSpec(memory_space=pl.ANY)
    f32, bf16 = jnp.float32, jnp.bfloat16
    left_piece = (seqs * group_c, chunks_c * tile_i)
    right_piece = (seqs * group_e, chunks_e * tile_j)
    dma = pltpu.SemaphoreType.DMA
    return pl.pallas_call(
        functools.partial(kernel, rows, cols),
        out_shape=(jax.ShapeDtypeStruct(a.shape, f32), jax.ShapeDtypeStruct(b.shape, f32)),
        in_specs=[vmem, vmem, anywhere, anywhere],
        out_specs=(vmem, vmem),
        scratch_shapes=[
            pltpu.VMEM((halves, rows) + a.shape, f32),
            pltpu.VMEM((rows,) + b.shape, f32),
            pltpu.VMEM((pairs, pair), f32),
            pltpu.VMEM(w.shape, f32),
            pltpu.VMEM((total * tile_i, LANES), f32),
            pltpu.VMEM((total * tile_i, LANES), f32),
            pltpu.VMEM((total * tile_j, LANES), f32),
            pltpu.VMEM((total * tile_j, LANES), f32),
            pltpu.VMEM((chunks_c, pairs, WIDE), bf16),
            pltpu.VMEM((chunks_c, pairs, WIDE), bf16),
            pltpu.VMEM((chunks_e, pairs, WIDE), bf16),
            pltpu.VMEM((chunks_e, pairs, WIDE), bf16),
            pltpu.VMEM((rows,) + left_piece, f32),
            pltpu.VMEM((rows,) + right_piece, f32),
            pltpu.VMEM((cols,) + left_piece, f32),
            pltpu.VMEM((rows,) + right_piece, f32),
            pltpu.VMEM(left_piece[::-1], f32),
            dma((2,)),
            dma((cols,)),
            dma((halves, rows)),
            dma((rows,)),
            dma((rows,)),
            dma((rows, halves)),
            dma((cols,)),
            dma((rows,)),
            dma((rows,)),
        ],
        compiler_params=pltpu.CompilerParams(
            collective_id=0, has_side_effects=True, vmem_limit_bytes=32 * 2**20),
    )(a, b, d.reshape(pairs, pair), w)


def solution(mesh):
    spec = P("row", "col", None)
    return jax.shard_map(
        functools.partial(on_device, mesh.shape["row"], mesh.shape["col"]),
        mesh=mesh,
        in_specs=(spec, spec, spec, P()),
        out_specs=(spec, spec),
        check_vma=False,
    )
```

```python
import functools

import jax
import jax.numpy as jnp
from jax import lax
from jax.experimental import pallas as pl
from jax.experimental.pallas import tpu as pltpu
from jax.sharding import PartitionSpec as P

MESH = pl.DeviceIdType.MESH
WIDE = 256
LANES = 128
DEPTH = 4


def split(x):
    high = x.astype(jnp.bfloat16)
    low = (x - high.astype(jnp.float32)).astype(jnp.bfloat16)
    return high, low


def dot_nt(x, y):
    return lax.dot_general(x, y, (((1,), (1,)), ((), ())), preferred_element_type=jnp.float32)


def kernel(
    rows, cols,
    a_hbm, b_hbm, d_hbm, w_hbm, left_ref, right_ref,
    a_own, b_own, a_pack, b_pack, a_all, b_all, d_buf, w_buf, a_high, a_low, b_high, b_low,
    g_high, g_low, h_high, h_low,
    left_sum, right_sum, left_send, right_send, left_recv, right_recv,
    local_sem, a_send_sem, a_recv_sem, b_send_sem, b_recv_sem,
    l_send_sem, l_recv_sem, r_send_sem, r_recv_sem,
):
    seqs, res, feats = a_hbm.shape
    feats_e = b_hbm.shape[2]
    tile_j = res
    tile_i = d_hbm.shape[0] // tile_j
    halves = tile_i // res
    total = seqs * rows
    group_c = WIDE // feats_e
    group_e = WIDE // feats
    chunks_c = feats // group_c
    chunks_e = feats_e // group_e

    r = lax.axis_index("row")
    q = lax.axis_index("col")
    owner_row = q // halves
    part = q % halves
    inside = owner_row == r

    copy_d = pltpu.make_async_copy(d_hbm, d_buf, local_sem.at[0])
    copy_w = pltpu.make_async_copy(w_hbm, w_buf, local_sem.at[1])
    fetch_a = pltpu.make_async_copy(a_hbm, a_own, local_sem.at[2])
    fetch_b = pltpu.make_async_copy(b_hbm, b_own, local_sem.at[3])
    fetch_b.start()
    fetch_a.start()
    copy_d.start()
    copy_w.start()

    barrier = pltpu.get_barrier_semaphore()

    def signal(row, col):
        pl.semaphore_signal(barrier, inc=1, device_id=(row, col), device_id_type=MESH)

    def unless_self(row, col, act, mine=None):
        same = jnp.logical_and(row == r, col == q)
        pl.when(jnp.logical_not(same))(act)
        if mine is not None:
            pl.when(same)(mine)

    for k in range(cols):
        unless_self(owner_row, k, functools.partial(signal, owner_row, k))
    for k in range(rows):
        for h in range(halves):
            col = r * halves + h
            unless_self(k, col, functools.partial(signal, k, col))
    for step in range(1, rows):
        signal((r + step) % rows, q)

    fetch_b.wait()
    b_pack[...] = jnp.concatenate([b_own[s] for s in range(seqs)], axis=1)
    b_all[r] = b_pack[...]
    fetch_a.wait()
    a_pack[...] = jnp.concatenate([a_own[s] for s in range(seqs)], axis=1)

    @pl.when(inside)
    def _():
        a_all[part, r] = a_pack[...]

    pl.semaphore_wait(barrier, (rows - 1) + 2 * jnp.where(inside, cols - 1, cols))

    def copy_b(step):
        dest = (r + step) % rows
        return pltpu.make_async_remote_copy(
            src_ref=b_pack, dst_ref=b_all.at[r], send_sem=b_send_sem.at[step],
            recv_sem=b_recv_sem.at[r], device_id=(dest, q), device_id_type=MESH)

    def copy_a(k):
        return pltpu.make_async_remote_copy(
            src_ref=a_pack, dst_ref=a_all.at[part, r], send_sem=a_send_sem.at[k],
            recv_sem=a_recv_sem.at[part, r], device_id=(owner_row, k), device_id_type=MESH)

    for step in range(1, rows):
        copy_b(step).start()
    for k in range(cols):
        unless_self(owner_row, k, lambda k=k: copy_a(k).start())

    copy_d.wait()
    copy_w.wait()
    d_plain = d_buf[...]
    d_turned = jnp.concatenate(
        [d_buf[pl.ds(j, tile_i, stride=tile_j), :] for j in range(tile_j)], axis=0)

    def expand(d, w, high_ref, low_ref, chunks):
        d_high, d_low = split(d)
        d_both = jnp.concatenate([d_high, d_low], axis=1)
        for n in range(chunks):
            w_high, w_low = split(w[n])
            out = dot_nt(d_both, jnp.concatenate([w_high, w_high], axis=1))
            out = out + dot_nt(d_high, w_low)
            out_high, out_low = split(out)
            high_ref[n] = out_high
            low_ref[n] = out_low

    expand(d_turned, [w_buf[n * WIDE:(n + 1) * WIDE, :] for n in range(chunks_c)],
           g_high, g_low, chunks_c)
    expand(d_plain, [jnp.concatenate(
        [w_buf[pl.ds(n * group_e + e, feats, stride=feats_e), :] for e in range(group_e)], axis=0)
        for n in range(chunks_e)], h_high, h_low, chunks_e)

    def repeat_lanes(x, width, high_ref, low_ref, base):
        size = x.shape[0]
        source = lax.broadcasted_iota(jnp.int32, (LANES, seqs * LANES), 0)
        target = lax.broadcasted_iota(jnp.int32, (LANES, seqs * LANES), 1)
        unit = (source == target // LANES * width + target % width).astype(jnp.bfloat16)
        for part_of, ref in zip(split(x), (high_ref, low_ref)):
            out = jnp.dot(part_of, unit, preferred_element_type=jnp.float32)
            for s in range(seqs):
                ref[base + s * size:base + (s + 1) * size, :] = out[:, s * LANES:(s + 1) * LANES]

    def masks(group, width):
        lane = lax.broadcasted_iota(jnp.int32, (group, WIDE), 1) // width
        block = lax.broadcasted_iota(jnp.int32, (group, WIDE), 0)
        return (lane == block).astype(jnp.float32).astype(jnp.bfloat16)

    def spread(ref, start, mask):
        x = ref[pl.ds(start, total, stride=res), :].astype(jnp.bfloat16)
        x = jnp.concatenate([x] * (WIDE // LANES), axis=1)
        return jnp.concatenate([x * mask[k:k + 1] for k in range(mask.shape[0])], axis=0)

    def contract(count, coef, mat):
        acc = None
        for first in range(0, count, DEPTH):
            steps = range(first, min(first + DEPTH, count))
            lhs = jnp.concatenate([coef(n) for n in steps], axis=1)
            rhs = jnp.concatenate([mat(n) for n in steps], axis=1)
            term = dot_nt(lhs, rhs)
            acc = term if acc is None else acc + term
        size, width = acc.shape[0] // 2, acc.shape[1] // 2
        return acc[:size, :width] + acc[:size, width:] + acc[size:, :width]

    def pieces(ref, k, group, parts, width):
        fold = LANES // width
        x = [ref[pl.ds(s * rows + k, group, stride=total), :] for s in range(seqs)]
        each = seqs // fold
        x = [jnp.concatenate(x[u * each:(u + 1) * each], axis=0) for u in range(fold)]
        return [jnp.concatenate([y[:, h * width:(h + 1) * width] for y in x], axis=1)
                for h in range(parts)]

    for step in range(1, rows):
        source = (r + step) % rows
        pltpu.make_async_remote_copy(
            src_ref=b_pack, dst_ref=b_all.at[source], send_sem=b_send_sem.at[step],
            recv_sem=b_recv_sem.at[source], device_id=(source, q), device_id_type=MESH).wait_recv()
    repeat_lanes(b_all[...].reshape(rows * res, LANES), feats_e, b_high, b_low, 0)
    mask_c = masks(group_c, feats_e)

    def left_coef(j):
        return jnp.concatenate([spread(b_high, j, mask_c), spread(b_low, j, mask_c)], axis=0)

    def left_mat(j):
        return jnp.concatenate(
            [ref[n, j * tile_i + h * res:j * tile_i + (h + 1) * res, :]
             for ref in (g_high, g_low) for h in range(halves) for n in range(chunks_c)], axis=0)

    left_sum[...] = contract(tile_j, left_coef, left_mat)
    for k in range(rows):
        for h, piece in enumerate(pieces(left_sum, k, group_c, halves, chunks_c * res)):
            left_send[k, h] = piece

    def copy_l(k, h):
        return pltpu.make_async_remote_copy(
            src_ref=left_send.at[k, h], dst_ref=left_recv.at[q], send_sem=l_send_sem.at[k, h],
            recv_sem=l_recv_sem.at[q], device_id=(k, r * halves + h), device_id_type=MESH)

    for k in range(rows):
        for h in range(halves):
            def mine(k=k, h=h):
                left_recv[q] = left_send[k, h]

            unless_self(k, r * halves + h, lambda k=k, h=h: copy_l(k, h).start(), mine)

    for k in range(rows):
        for h in range(halves):
            def arrive(k=k, h=h):
                pltpu.make_async_remote_copy(
                    src_ref=a_pack, dst_ref=a_all.at[h, k], send_sem=a_send_sem.at[0],
                    recv_sem=a_recv_sem.at[h, k], device_id=(k, r * halves + h),
                    device_id_type=MESH).wait_recv()

            unless_self(k, r * halves + h, arrive)
    for h in range(halves):
        repeat_lanes(a_all[h].reshape(rows * res, LANES), feats, a_high, a_low, h * total * res)
    mask_e = masks(group_e, feats)

    def right_coef(i):
        start = (i // res) * total * res + i % res
        return jnp.concatenate([spread(a_high, start, mask_e), spread(a_low, start, mask_e)], axis=0)

    def right_mat(i):
        span = slice(i * tile_j, (i + 1) * tile_j)
        return jnp.concatenate(
            [ref[n, span, :] for ref in (h_high, h_low) for n in range(chunks_e)], axis=0)

    right = contract(tile_i, right_coef, right_mat)
    right_sum[...] = jnp.concatenate([right] * (LANES // right.shape[1]), axis=1)
    for k in range(rows):
        right_send[k] = pieces(right_sum, k, group_e, 1, chunks_e * tile_j)[0]
    right_recv[r] = right_send[r]

    def copy_r(step):
        dest = (r + step) % rows
        return pltpu.make_async_remote_copy(
            src_ref=right_send.at[dest], dst_ref=right_recv.at[r], send_sem=r_send_sem.at[step],
            recv_sem=r_recv_sem.at[r], device_id=(dest, q), device_id_type=MESH)

    for step in range(1, rows):
        copy_r(step).start()

    for k in range(cols):
        def arrive(k=k):
            pltpu.make_async_remote_copy(
                src_ref=left_send.at[0, 0], dst_ref=left_recv.at[k], send_sem=l_send_sem.at[0, 0],
                recv_sem=l_recv_sem.at[k], device_id=(owner_row, k),
                device_id_type=MESH).wait_recv()

        unless_self(owner_row, k, arrive)
    left_ref[...] = jnp.sum(left_recv[...], axis=0) / total

    for step in range(1, rows):
        source = (r + step) % rows
        pltpu.make_async_remote_copy(
            src_ref=right_send.at[source], dst_ref=right_recv.at[source],
            send_sem=r_send_sem.at[step], recv_sem=r_recv_sem.at[source],
            device_id=(source, q), device_id_type=MESH).wait_recv()
    right_ref[...] = jnp.sum(right_recv[...], axis=0) / total

    for step in range(1, rows):
        copy_b(step).wait_send()
        copy_r(step).wait_send()
    for k in range(cols):
        unless_self(owner_row, k, lambda k=k: copy_a(k).wait_send())
    for k in range(rows):
        for h in range(halves):
            unless_self(k, r * halves + h, lambda k=k, h=h: copy_l(k, h).wait_send())


def unfold(group_c, group_e, left_ref, right_ref, left_out, right_out):
    for group, ref, out in ((group_c, left_ref, left_out), (group_e, right_ref, right_out)):
        seqs, res, feats = out.shape
        x = ref[...].T
        each = ref.shape[0] // group
        chunks = feats // group
        for s in range(seqs):
            u, v = s // each, s % each
            out[s] = jnp.concatenate(
                [x[(u * chunks + n) * res:(u * chunks + n + 1) * res, v * group:(v + 1) * group]
                 for n in range(chunks)], axis=1)


def on_device(rows, cols, a, b, d, w):
    seqs, res, feats = a.shape
    feats_e = b.shape[2]
    tile_i, tile_j, pair = d.shape
    halves = tile_i // res
    total = seqs * rows
    group_c, group_e = WIDE // feats_e, WIDE // feats
    chunks_c, chunks_e = feats // group_c, feats_e // group_e
    pairs = tile_i * tile_j
    vmem = pl.BlockSpec(memory_space=pltpu.VMEM)
    hbm = pl.BlockSpec(memory_space=pltpu.HBM)
    f32, bf16 = jnp.float32, jnp.bfloat16
    left_piece = (seqs * feats * res // LANES, LANES)
    right_piece = (seqs * feats_e * res // LANES, LANES)
    dma = pltpu.SemaphoreType.DMA
    left, right = pl.pallas_call(
        functools.partial(kernel, rows, cols),
        out_shape=(jax.ShapeDtypeStruct(left_piece, f32), jax.ShapeDtypeStruct(right_piece, f32)),
        in_specs=[hbm] * 4,
        out_specs=(vmem, vmem),
        scratch_shapes=[
            pltpu.VMEM(a.shape, f32),
            pltpu.VMEM(b.shape, f32),
            pltpu.VMEM((res, LANES), f32),
            pltpu.VMEM((res, LANES), f32),
            pltpu.VMEM((halves, rows, res, LANES), f32),
            pltpu.VMEM((rows, res, LANES), f32),
            pltpu.VMEM((pairs, pair), f32),
            pltpu.VMEM(w.shape, f32),
            pltpu.VMEM((total * tile_i, LANES), f32),
            pltpu.VMEM((total * tile_i, LANES), f32),
            pltpu.VMEM((total * tile_j, LANES), f32),
            pltpu.VMEM((total * tile_j, LANES), f32),
            pltpu.VMEM((chunks_c, pairs, WIDE), bf16),
            pltpu.VMEM((chunks_c, pairs, WIDE), bf16),
            pltpu.VMEM((chunks_e, pairs, WIDE), bf16),
            pltpu.VMEM((chunks_e, pairs, WIDE), bf16),
            pltpu.VMEM((total * group_c, LANES), f32),
            pltpu.VMEM((total * group_e, LANES), f32),
            pltpu.VMEM((rows, halves) + left_piece, f32),
            pltpu.VMEM((rows,) + right_piece, f32),
            pltpu.VMEM((cols,) + left_piece, f32),
            pltpu.VMEM((rows,) + right_piece, f32),
            dma((4,)),
            dma((cols,)),
            dma((halves, rows)),
            dma((rows,)),
            dma((rows,)),
            dma((rows, halves)),
            dma((cols,)),
            dma((rows,)),
            dma((rows,)),
        ],
        compiler_params=pltpu.CompilerParams(
            collective_id=0, has_side_effects=True, vmem_limit_bytes=54 * 2**20 - 101 * 2**10),
    )(a, b, d.reshape(pairs, pair), w)
    return pl.pallas_call(
        functools.partial(unfold, group_c, group_e),
        out_shape=(jax.ShapeDtypeStruct(a.shape, f32), jax.ShapeDtypeStruct(b.shape, f32)),
        in_specs=[vmem] * 2,
        out_specs=(vmem, vmem),
    )(left, right)


def solution(mesh):
    spec = P("row", "col", None)
    return jax.shard_map(
        functools.partial(on_device, mesh.shape["row"], mesh.shape["col"]),
        mesh=mesh,
        in_specs=(spec, spec, spec, P()),
        out_specs=(spec, spec),
        check_vma=False,
    )
```

```python
import functools

import jax
import jax.numpy as jnp
from jax import lax
from jax.experimental import pallas as pl
from jax.experimental.pallas import tpu as pltpu
from jax.sharding import PartitionSpec as P

MESH = pl.DeviceIdType.MESH
WIDE = 256
LANES = 128
DEPTH = 4


def split(x):
    high = x.astype(jnp.bfloat16)
    low = (x - high.astype(jnp.float32)).astype(jnp.bfloat16)
    return high, low


def dot_nt(x, y):
    return lax.dot_general(x, y, (((1,), (1,)), ((), ())), preferred_element_type=jnp.float32)


def kernel(
    rows, cols,
    a_hbm, b_hbm, d_hbm, w_hbm, out_ref,
    a_own, b_own, a_pack, b_pack, a_all, b_all, d_buf, w_buf, a_high, a_low, b_high, b_low,
    g_high, g_low, h_high, h_low,
    left_sum, right_sum, left_send, right_send, left_recv, right_recv,
    local_sem, a_send_sem, a_recv_sem, b_send_sem, b_recv_sem,
    l_send_sem, l_recv_sem, r_send_sem, r_recv_sem,
):
    seqs, res, feats = a_hbm.shape
    feats_e = b_hbm.shape[2]
    tile_j = res
    tile_i = d_hbm.shape[0] // tile_j
    halves = tile_i // res
    total = seqs * rows
    group_c = WIDE // feats_e
    group_e = WIDE // feats
    chunks_c = feats // group_c
    chunks_e = feats_e // group_e

    r = lax.axis_index("row")
    q = lax.axis_index("col")
    owner_row = q // halves
    part = q % halves
    inside = owner_row == r

    copy_d = pltpu.make_async_copy(d_hbm, d_buf, local_sem.at[0])
    copy_w = pltpu.make_async_copy(w_hbm, w_buf, local_sem.at[1])
    fetch_a = pltpu.make_async_copy(a_hbm, a_own, local_sem.at[2])
    fetch_b = pltpu.make_async_copy(b_hbm, b_own, local_sem.at[3])
    fetch_b.start()
    fetch_a.start()
    copy_d.start()
    copy_w.start()

    barrier = pltpu.get_barrier_semaphore()

    def signal(row, col):
        pl.semaphore_signal(barrier, inc=1, device_id=(row, col), device_id_type=MESH)

    def arrived(ref, sem):
        pltpu.make_async_copy(ref, ref, sem).wait()

    def owners(act, own):
        for step in range(1, cols):
            act((q + step) % cols, 0)
        pl.when(jnp.logical_not(inside))(lambda: act(q, 1))
        if own is not None:
            pl.when(inside)(own)

    def sources(act, own):
        for step in range(1, rows):
            for h in range(halves):
                act((r + step) % rows, h, 0)
        for step in range(1, halves):
            act(r, (part + step) % halves, 0)
        pl.when(jnp.logical_not(inside))(lambda: act(r, part, 1))
        if own is not None:
            pl.when(inside)(own)

    owners(lambda col, _: signal(owner_row, col), None)
    sources(lambda row, h, _: signal(row, r * halves + h), None)
    for step in range(1, rows):
        signal((r + step) % rows, q)

    fetch_b.wait()
    b_pack[...] = jnp.concatenate([b_own[s] for s in range(seqs)], axis=1)
    fetch_a.wait()
    a_pack[...] = jnp.concatenate([a_own[s] for s in range(seqs)], axis=1)

    pl.semaphore_wait(barrier, (rows - 1) + 2 * jnp.where(inside, cols - 1, cols))

    for step in range(1, rows):
        pltpu.make_async_remote_copy(
            src_ref=b_pack, dst_ref=b_all.at[r], send_sem=b_send_sem, recv_sem=b_recv_sem,
            device_id=((r + step) % rows, q), device_id_type=MESH).start()
    pltpu.make_async_copy(b_pack, b_all.at[r], b_recv_sem).start()

    def send_a(col, which):
        pltpu.make_async_remote_copy(
            src_ref=a_pack, dst_ref=a_all.at[part, r], send_sem=a_send_sem.at[which],
            recv_sem=a_recv_sem, device_id=(owner_row, col), device_id_type=MESH).start()

    owners(send_a, lambda: pltpu.make_async_copy(a_pack, a_all.at[part, r], a_recv_sem).start())

    copy_d.wait()
    copy_w.wait()
    d_plain = d_buf[...]
    d_turned = jnp.concatenate(
        [d_buf[pl.ds(j, tile_i, stride=tile_j), :] for j in range(tile_j)], axis=0)

    def expand(d, w, high_ref, low_ref, chunks):
        d_high, d_low = split(d)
        d_both = jnp.concatenate([d_high, d_low], axis=1)
        for n in range(chunks):
            w_high, w_low = split(w[n])
            out = dot_nt(d_both, jnp.concatenate([w_high, w_high], axis=1))
            out = out + dot_nt(d_high, w_low)
            out_high, out_low = split(out)
            high_ref[n] = out_high
            low_ref[n] = out_low

    expand(d_turned, [w_buf[n * WIDE:(n + 1) * WIDE, :] for n in range(chunks_c)],
           g_high, g_low, chunks_c)
    expand(d_plain, [jnp.concatenate(
        [w_buf[pl.ds(n * group_e + e, feats, stride=feats_e), :] for e in range(group_e)], axis=0)
        for n in range(chunks_e)], h_high, h_low, chunks_e)

    def repeat_lanes(x, width, high_ref, low_ref, base):
        size = x.shape[0]
        source = lax.broadcasted_iota(jnp.int32, (LANES, seqs * LANES), 0)
        target = lax.broadcasted_iota(jnp.int32, (LANES, seqs * LANES), 1)
        unit = (source == target // LANES * width + target % width).astype(jnp.bfloat16)
        for part_of, ref in zip(split(x), (high_ref, low_ref)):
            out = jnp.dot(part_of, unit, preferred_element_type=jnp.float32)
            for s in range(seqs):
                ref[base + s * size:base + (s + 1) * size, :] = out[:, s * LANES:(s + 1) * LANES]

    def masks(group, width):
        lane = lax.broadcasted_iota(jnp.int32, (group, WIDE), 1) // width
        block = lax.broadcasted_iota(jnp.int32, (group, WIDE), 0)
        return (lane == block).astype(jnp.float32).astype(jnp.bfloat16)

    def spread(ref, start, mask):
        x = ref[pl.ds(start, total, stride=res), :].astype(jnp.bfloat16)
        x = jnp.concatenate([x] * (WIDE // LANES), axis=1)
        return jnp.concatenate([x * mask[k:k + 1] for k in range(mask.shape[0])], axis=0)

    def contract(count, coef, mat):
        acc = None
        for first in range(0, count, DEPTH):
            steps = range(first, min(first + DEPTH, count))
            lhs = jnp.concatenate([coef(n) for n in steps], axis=1)
            rhs = jnp.concatenate([mat(n) for n in steps], axis=1)
            term = dot_nt(lhs, rhs)
            acc = term if acc is None else acc + term
        size, width = acc.shape[0] // 2, acc.shape[1] // 2
        return acc[:size, :width] + acc[:size, width:] + acc[size:, :width]

    def pieces(ref, k, group, parts, width):
        fold = LANES // width
        x = [ref[pl.ds(s * rows + k, group, stride=total), :] for s in range(seqs)]
        each = seqs // fold
        x = [jnp.concatenate(x[u * each:(u + 1) * each], axis=0) for u in range(fold)]
        return [jnp.concatenate([y[:, h * width:(h + 1) * width] for y in x], axis=1)
                for h in range(parts)]

    arrived(b_all, b_recv_sem)
    repeat_lanes(b_all[...].reshape(rows * res, LANES), feats_e, b_high, b_low, 0)
    mask_c = masks(group_c, feats_e)

    def left_coef(j):
        return jnp.concatenate([spread(b_high, j, mask_c), spread(b_low, j, mask_c)], axis=0)

    def left_mat(j):
        return jnp.concatenate(
            [ref[n, j * tile_i + h * res:j * tile_i + (h + 1) * res, :]
             for ref in (g_high, g_low) for h in range(halves) for n in range(chunks_c)], axis=0)

    left_sum[...] = contract(tile_j, left_coef, left_mat)
    for k in range(rows):
        for h, piece in enumerate(pieces(left_sum, k, group_c, halves, chunks_c * res)):
            left_send[k, h] = piece

    def send_l(row, h, which):
        pltpu.make_async_remote_copy(
            src_ref=left_send.at[row, h], dst_ref=left_recv.at[q], send_sem=l_send_sem.at[which],
            recv_sem=l_recv_sem, device_id=(row, r * halves + h), device_id_type=MESH).start()

    sources(send_l, lambda: pltpu.make_async_copy(
        left_send.at[r, part], left_recv.at[q], l_recv_sem).start())

    arrived(a_all, a_recv_sem)
    for h in range(halves):
        repeat_lanes(a_all[h].reshape(rows * res, LANES), feats, a_high, a_low, h * total * res)
    mask_e = masks(group_e, feats)

    def right_coef(i):
        start = (i // res) * total * res + i % res
        return jnp.concatenate([spread(a_high, start, mask_e), spread(a_low, start, mask_e)], axis=0)

    def right_mat(i):
        span = slice(i * tile_j, (i + 1) * tile_j)
        return jnp.concatenate(
            [ref[n, span, :] for ref in (h_high, h_low) for n in range(chunks_e)], axis=0)

    right = contract(tile_i, right_coef, right_mat)
    right_sum[...] = jnp.concatenate([right] * (LANES // right.shape[1]), axis=1)
    for k in range(rows):
        right_send[k] = pieces(right_sum, k, group_e, 1, chunks_e * tile_j)[0]
    for step in range(1, rows):
        dest = (r + step) % rows
        pltpu.make_async_remote_copy(
            src_ref=right_send.at[dest], dst_ref=right_recv.at[r], send_sem=r_send_sem,
            recv_sem=r_recv_sem, device_id=(dest, q), device_id_type=MESH).start()
    pltpu.make_async_copy(right_send.at[r], right_recv.at[r], r_recv_sem).start()

    arrived(left_recv, l_recv_sem)
    size = left_recv.shape[1]
    out_ref[:size, :] = jnp.sum(left_recv[...], axis=0) / total
    arrived(right_recv, r_recv_sem)
    out_ref[size:, :] = jnp.sum(right_recv[...], axis=0) / total

    arrived(b_all.at[pl.ds(0, rows - 1)], b_send_sem)
    arrived(right_recv.at[pl.ds(0, rows - 1)], r_send_sem)
    arrived(left_recv.at[pl.ds(0, cols - 1)], l_send_sem.at[0])
    arrived(d_buf.at[pl.ds(0, (cols - 1) * res)], a_send_sem.at[0])

    @pl.when(jnp.logical_not(inside))
    def _():
        arrived(left_recv.at[0], l_send_sem.at[1])
        arrived(a_pack, a_send_sem.at[1])


def unfold(group_c, group_e, sums_ref, left_out, right_out):
    size = left_out.size // LANES
    for group, ref, out in (
        (group_c, sums_ref.at[:size], left_out), (group_e, sums_ref.at[size:], right_out)
    ):
        seqs, res, feats = out.shape
        x = ref[...].T
        each = ref.shape[0] // group
        chunks = feats // group
        for s in range(seqs):
            u, v = s // each, s % each
            out[s] = jnp.concatenate(
                [x[(u * chunks + n) * res:(u * chunks + n + 1) * res, v * group:(v + 1) * group]
                 for n in range(chunks)], axis=1)


def on_device(rows, cols, a, b, d, w):
    seqs, res, feats = a.shape
    feats_e = b.shape[2]
    tile_i, tile_j, pair = d.shape
    halves = tile_i // res
    total = seqs * rows
    group_c, group_e = WIDE // feats_e, WIDE // feats
    chunks_c, chunks_e = feats // group_c, feats_e // group_e
    pairs = tile_i * tile_j
    vmem = pl.BlockSpec(memory_space=pltpu.VMEM)
    hbm = pl.BlockSpec(memory_space=pltpu.HBM)
    f32, bf16 = jnp.float32, jnp.bfloat16
    left_piece = (seqs * feats * res // LANES, LANES)
    right_piece = (seqs * feats_e * res // LANES, LANES)
    dma = pltpu.SemaphoreType.DMA
    sums = pl.pallas_call(
        functools.partial(kernel, rows, cols),
        out_shape=jax.ShapeDtypeStruct((left_piece[0] + right_piece[0], LANES), f32),
        in_specs=[hbm] * 4,
        out_specs=vmem,
        scratch_shapes=[
            pltpu.VMEM(a.shape, f32),
            pltpu.VMEM(b.shape, f32),
            pltpu.VMEM((res, LANES), f32),
            pltpu.VMEM((res, LANES), f32),
            pltpu.VMEM((halves, rows, res, LANES), f32),
            pltpu.VMEM((rows, res, LANES), f32),
            pltpu.VMEM((pairs, pair), f32),
            pltpu.VMEM(w.shape, f32),
            pltpu.VMEM((total * tile_i, LANES), f32),
            pltpu.VMEM((total * tile_i, LANES), f32),
            pltpu.VMEM((total * tile_j, LANES), f32),
            pltpu.VMEM((total * tile_j, LANES), f32),
            pltpu.VMEM((chunks_c, pairs, WIDE), bf16),
            pltpu.VMEM((chunks_c, pairs, WIDE), bf16),
            pltpu.VMEM((chunks_e, pairs, WIDE), bf16),
            pltpu.VMEM((chunks_e, pairs, WIDE), bf16),
            pltpu.VMEM((total * group_c, LANES), f32),
            pltpu.VMEM((total * group_e, LANES), f32),
            pltpu.VMEM((rows, halves) + left_piece, f32),
            pltpu.VMEM((rows,) + right_piece, f32),
            pltpu.VMEM((cols,) + left_piece, f32),
            pltpu.VMEM((rows,) + right_piece, f32),
            dma((4,)),
            dma((2,)),
            dma(()),
            dma(()),
            dma(()),
            dma((2,)),
            dma(()),
            dma(()),
            dma(()),
        ],
        compiler_params=pltpu.CompilerParams(
            collective_id=0, has_side_effects=True, vmem_limit_bytes=54 * 2**20 - 117 * 2**10),
    )(a, b, d.reshape(pairs, pair), w)
    return pl.pallas_call(
        functools.partial(unfold, group_c, group_e),
        out_shape=(jax.ShapeDtypeStruct(a.shape, f32), jax.ShapeDtypeStruct(b.shape, f32)),
        in_specs=[vmem],
        out_specs=(vmem, vmem),
    )(sums)


def solution(mesh):
    spec = P("row", "col", None)
    return jax.shard_map(
        functools.partial(on_device, mesh.shape["row"], mesh.shape["col"]),
        mesh=mesh,
        in_specs=(spec, spec, spec, P()),
        out_specs=(spec, spec),
        check_vma=False,
    )
```

```python
import functools

import jax
import jax.numpy as jnp
from jax import lax
from jax.experimental import pallas as pl
from jax.experimental.pallas import tpu as pltpu
from jax.sharding import PartitionSpec as P

MESH = pl.DeviceIdType.MESH
WIDE = 128
SPAN = 2
LANES = 128
DEPTH = 8


def split(x):
    high = x.astype(jnp.bfloat16)
    low = (x - high.astype(jnp.float32)).astype(jnp.bfloat16)
    return high, low


def dot_nt(x, y):
    return lax.dot_general(x, y, (((1,), (1,)), ((), ())), preferred_element_type=jnp.float32)


def kernel(
    rows, cols,
    a_hbm, b_hbm, d_hbm, w_hbm, out_ref,
    a_own, b_own, a_pack, b_pack, a_all, b_all, d_buf, w_buf, a_high, a_low, b_high, b_low,
    g_buf, h_buf,
    left_sum, right_sum, left_send, right_send, left_recv, right_recv,
    local_sem, a_send_sem, a_recv_sem, b_send_sem, b_recv_sem,
    l_send_sem, l_recv_sem, r_send_sem, r_recv_sem,
):
    seqs, res, feats = a_hbm.shape
    feats_e = b_hbm.shape[2]
    tile_j = res
    tile_i = d_hbm.shape[0] // tile_j
    halves = tile_i // res
    total = seqs * rows
    group_c = WIDE // feats_e
    group_e = WIDE // feats
    chunks_c = feats // group_c
    chunks_e = feats_e // group_e

    r = lax.axis_index("row")
    q = lax.axis_index("col")
    owner_row = q // halves
    part = q % halves
    inside = owner_row == r

    copy_d = pltpu.make_async_copy(d_hbm, d_buf, local_sem.at[0])
    copy_w = pltpu.make_async_copy(w_hbm, w_buf, local_sem.at[1])
    fetch_a = pltpu.make_async_copy(a_hbm, a_own, local_sem.at[2])
    fetch_b = pltpu.make_async_copy(b_hbm, b_own, local_sem.at[3])
    fetch_b.start()
    fetch_a.start()
    copy_d.start()
    copy_w.start()

    barrier = pltpu.get_barrier_semaphore()

    def signal(row, col):
        pl.semaphore_signal(barrier, inc=1, device_id=(row, col), device_id_type=MESH)

    def arrived(ref, sem):
        pltpu.make_async_copy(ref, ref, sem).wait()

    def owners(act, own):
        for step in range(1, cols):
            act((q + step) % cols, 0)
        pl.when(jnp.logical_not(inside))(lambda: act(q, 1))
        if own is not None:
            pl.when(inside)(own)

    def sources(act, own):
        for step in range(1, rows):
            for h in range(halves):
                act((r + step) % rows, h, 0)
        for step in range(1, halves):
            act(r, (part + step) % halves, 0)
        pl.when(jnp.logical_not(inside))(lambda: act(r, part, 1))
        if own is not None:
            pl.when(inside)(own)

    owners(lambda col, _: signal(owner_row, col), None)
    sources(lambda row, h, _: signal(row, r * halves + h), None)
    for step in range(1, rows):
        signal((r + step) % rows, q)

    fetch_b.wait()
    b_pack[...] = jnp.concatenate([b_own[s] for s in range(seqs)], axis=1)
    fetch_a.wait()
    a_pack[...] = jnp.concatenate([a_own[s] for s in range(seqs)], axis=1)

    pl.semaphore_wait(barrier, (rows - 1) + 2 * jnp.where(inside, cols - 1, cols))

    for step in range(1, rows):
        pltpu.make_async_remote_copy(
            src_ref=b_pack, dst_ref=b_all.at[r], send_sem=b_send_sem, recv_sem=b_recv_sem,
            device_id=((r + step) % rows, q), device_id_type=MESH).start()
    pltpu.make_async_copy(b_pack, b_all.at[r], b_recv_sem).start()

    def send_a(col, which):
        pltpu.make_async_remote_copy(
            src_ref=a_pack, dst_ref=a_all.at[part, r], send_sem=a_send_sem.at[which],
            recv_sem=a_recv_sem, device_id=(owner_row, col), device_id_type=MESH).start()

    owners(send_a, lambda: pltpu.make_async_copy(a_pack, a_all.at[part, r], a_recv_sem).start())

    copy_d.wait()
    copy_w.wait()
    d_plain = d_buf[...]
    d_turned = jnp.concatenate(
        [d_buf[pl.ds(j, tile_i, stride=tile_j), :] for j in range(tile_j)], axis=0)

    def expand(d, w, chunks, place):
        d_high, d_low = split(d)
        d_all = jnp.concatenate([d_high, d_low, d_high], axis=1)
        for first in range(0, chunks, SPAN):
            group = range(first, min(first + SPAN, chunks))
            w_high, w_low = split(jnp.concatenate([w(n) for n in group], axis=0))
            out = dot_nt(d_all, jnp.concatenate([w_high, w_high, w_low], axis=1))
            for low, value in enumerate(split(out)):
                for n in group:
                    place(low, n, value[:, (n - first) * WIDE:(n - first + 1) * WIDE])

    def place_g(low, n, value):
        for j in range(tile_j):
            for h in range(halves):
                top = ((low * halves + h) * chunks_c + n) * res
                g_buf[top:top + res, j * WIDE:(j + 1) * WIDE] = value[
                    j * tile_i + h * res:j * tile_i + (h + 1) * res]

    def place_h(low, n, value):
        top = (low * chunks_e + n) * tile_j
        for i in range(tile_i):
            h_buf[top:top + tile_j, i * WIDE:(i + 1) * WIDE] = value[i * tile_j:(i + 1) * tile_j]

    expand(d_turned, lambda n: w_buf[n * WIDE:(n + 1) * WIDE, :], chunks_c, place_g)
    expand(d_plain, lambda n: jnp.concatenate(
        [w_buf[pl.ds(n * group_e + e, feats, stride=feats_e), :] for e in range(group_e)], axis=0),
        chunks_e, place_h)

    def repeat_lanes(x, width, high_ref, low_ref, base):
        size = x.shape[0]
        source = lax.broadcasted_iota(jnp.int32, (LANES, seqs * LANES), 0)
        target = lax.broadcasted_iota(jnp.int32, (LANES, seqs * LANES), 1)
        unit = (source == target // LANES * width + target % width).astype(jnp.bfloat16)
        for part_of, ref in zip(split(x), (high_ref, low_ref)):
            out = jnp.dot(part_of, unit, preferred_element_type=jnp.float32)
            for s in range(seqs):
                ref[base + s * size:base + (s + 1) * size, :] = out[:, s * LANES:(s + 1) * LANES]

    def masks(group, width):
        lane = lax.broadcasted_iota(jnp.int32, (group, WIDE), 1) // width
        block = lax.broadcasted_iota(jnp.int32, (group, WIDE), 0)
        return (lane == block).astype(jnp.float32).astype(jnp.bfloat16)

    def spread(ref, start, mask):
        x = ref[pl.ds(start, total, stride=res), :].astype(jnp.bfloat16)
        return jnp.concatenate([x * mask[k:k + 1] for k in range(mask.shape[0])], axis=0)

    def contract(count, coef, mat):
        acc = None
        for first in range(0, count, DEPTH):
            last = min(first + DEPTH, count)
            lhs = jnp.concatenate([coef(n) for n in range(first, last)], axis=1)
            term = dot_nt(lhs, mat[:, first * WIDE:last * WIDE])
            acc = term if acc is None else acc + term
        size, width = acc.shape[0] // 2, acc.shape[1] // 2
        return acc[:size, :width] + acc[:size, width:] + acc[size:, :width]

    def piece(ref, k, group):
        return jnp.concatenate(
            [ref[pl.ds(s * rows + k, group, stride=total), :] for s in range(seqs)], axis=0)

    arrived(b_all, b_recv_sem)
    repeat_lanes(b_all[...].reshape(rows * res, LANES), feats_e, b_high, b_low, 0)
    mask_c = masks(group_c, feats_e)

    def left_coef(j):
        return jnp.concatenate([spread(b_high, j, mask_c), spread(b_low, j, mask_c)], axis=0)

    left = contract(tile_j, left_coef, g_buf)
    for h in range(halves):
        left_sum[h] = left[:, h * LANES:(h + 1) * LANES]
    for k in range(rows):
        for h in range(halves):
            left_send[k, h] = piece(left_sum.at[h], k, group_c)

    def send_l(row, h, which):
        pltpu.make_async_remote_copy(
            src_ref=left_send.at[row, h], dst_ref=left_recv.at[q], send_sem=l_send_sem.at[which],
            recv_sem=l_recv_sem, device_id=(row, r * halves + h), device_id_type=MESH).start()

    sources(send_l, lambda: pltpu.make_async_copy(
        left_send.at[r, part], left_recv.at[q], l_recv_sem).start())

    arrived(a_all, a_recv_sem)
    for h in range(halves):
        repeat_lanes(a_all[h].reshape(rows * res, LANES), feats, a_high, a_low, h * total * res)
    mask_e = masks(group_e, feats)

    def right_coef(i):
        start = (i // res) * total * res + i % res
        return jnp.concatenate([spread(a_high, start, mask_e), spread(a_low, start, mask_e)], axis=0)

    right_sum[...] = contract(tile_i, right_coef, h_buf)
    for k in range(rows):
        right_send[k] = piece(right_sum, k, group_e)

    for step in range(1, rows):
        dest = (r + step) % rows
        pltpu.make_async_remote_copy(
            src_ref=right_send.at[dest], dst_ref=right_recv.at[r], send_sem=r_send_sem,
            recv_sem=r_recv_sem, device_id=(dest, q), device_id_type=MESH).start()
    pltpu.make_async_copy(right_send.at[r], right_recv.at[r], r_recv_sem).start()

    arrived(left_recv, l_recv_sem)
    size = left_recv.shape[1]
    out_ref[:size, :] = jnp.sum(left_recv[...], axis=0) / total
    arrived(right_recv, r_recv_sem)
    out_ref[size:, :] = jnp.sum(right_recv[...], axis=0) / total

    arrived(b_all.at[pl.ds(0, rows - 1)], b_send_sem)
    arrived(right_recv.at[pl.ds(0, rows - 1)], r_send_sem)
    arrived(left_recv.at[pl.ds(0, cols - 1)], l_send_sem.at[0])
    arrived(d_buf.at[pl.ds(0, (cols - 1) * res)], a_send_sem.at[0])

    @pl.when(jnp.logical_not(inside))
    def _():
        arrived(left_recv.at[0], l_send_sem.at[1])
        arrived(a_pack, a_send_sem.at[1])


def unfold(group_c, group_e, sums_ref, left_out, right_out):
    size = left_out.size // LANES
    for group, ref, out in (
        (group_c, sums_ref.at[:size], left_out), (group_e, sums_ref.at[size:], right_out)
    ):
        seqs, res, feats = out.shape
        x = ref[...].T
        each = ref.shape[0] // group
        chunks = feats // group
        for s in range(seqs):
            u, v = s // each, s % each
            out[s] = jnp.concatenate(
                [x[(u * chunks + n) * res:(u * chunks + n + 1) * res, v * group:(v + 1) * group]
                 for n in range(chunks)], axis=1)


def on_device(rows, cols, a, b, d, w):
    seqs, res, feats = a.shape
    feats_e = b.shape[2]
    tile_i, tile_j, pair = d.shape
    halves = tile_i // res
    total = seqs * rows
    group_c, group_e = WIDE // feats_e, WIDE // feats
    chunks_c, chunks_e = feats // group_c, feats_e // group_e
    pairs = tile_i * tile_j
    vmem = pl.BlockSpec(memory_space=pltpu.VMEM)
    hbm = pl.BlockSpec(memory_space=pltpu.HBM)
    f32, bf16 = jnp.float32, jnp.bfloat16
    left_piece = (seqs * feats * res // LANES, LANES)
    right_piece = (seqs * feats_e * res // LANES, LANES)
    dma = pltpu.SemaphoreType.DMA
    sums = pl.pallas_call(
        functools.partial(kernel, rows, cols),
        out_shape=jax.ShapeDtypeStruct((left_piece[0] + right_piece[0], LANES), f32),
        in_specs=[hbm] * 4,
        out_specs=vmem,
        scratch_shapes=[
            pltpu.VMEM(a.shape, f32),
            pltpu.VMEM(b.shape, f32),
            pltpu.VMEM((res, LANES), f32),
            pltpu.VMEM((res, LANES), f32),
            pltpu.VMEM((halves, rows, res, LANES), f32),
            pltpu.VMEM((rows, res, LANES), f32),
            pltpu.VMEM((pairs, pair), f32),
            pltpu.VMEM(w.shape, f32),
            pltpu.VMEM((total * tile_i, LANES), f32),
            pltpu.VMEM((total * tile_i, LANES), f32),
            pltpu.VMEM((total * tile_j, LANES), f32),
            pltpu.VMEM((total * tile_j, LANES), f32),
            pltpu.VMEM((2 * chunks_c * tile_i, tile_j * WIDE), bf16),
            pltpu.VMEM((2 * chunks_e * tile_j, tile_i * WIDE), bf16),
            pltpu.VMEM((halves, total * group_c, LANES), f32),
            pltpu.VMEM((total * group_e, LANES), f32),
            pltpu.VMEM((rows, halves) + left_piece, f32),
            pltpu.VMEM((rows,) + right_piece, f32),
            pltpu.VMEM((cols,) + left_piece, f32),
            pltpu.VMEM((rows,) + right_piece, f32),
            dma((4,)),
            dma((2,)),
            dma(()),
            dma(()),
            dma(()),
            dma((2,)),
            dma(()),
            dma(()),
            dma(()),
        ],
        compiler_params=pltpu.CompilerParams(
            collective_id=0, has_side_effects=True, vmem_limit_bytes=60 * 2**20),
    )(a, b, d.reshape(pairs, pair), w)
    return pl.pallas_call(
        functools.partial(unfold, group_c, group_e),
        out_shape=(jax.ShapeDtypeStruct(a.shape, f32), jax.ShapeDtypeStruct(b.shape, f32)),
        in_specs=[vmem],
        out_specs=(vmem, vmem),
    )(sums)


def solution(mesh):
    spec = P("row", "col", None)
    return jax.shard_map(
        functools.partial(on_device, mesh.shape["row"], mesh.shape["col"]),
        mesh=mesh,
        in_specs=(spec, spec, spec, P()),
        out_specs=(spec, spec),
        check_vma=False,
    )
```

```python
import functools

import jax
import jax.numpy as jnp
from jax import lax
from jax.experimental import pallas as pl
from jax.experimental.pallas import tpu as pltpu
from jax.sharding import PartitionSpec as P

MESH = pl.DeviceIdType.MESH
WIDE = 128
SPAN = 2
LANES = 128
DEPTH = 8


def split(x):
    high = x.astype(jnp.bfloat16)
    low = (x - high.astype(jnp.float32)).astype(jnp.bfloat16)
    return high, low


def dot_nt(x, y):
    return lax.dot_general(x, y, (((1,), (1,)), ((), ())), preferred_element_type=jnp.float32)


def kernel(
    rows, cols,
    a_hbm, b_hbm, d_hbm, w_hbm, out_ref,
    a_own, b_own, a_pack, b_pack, a_all, b_all, d_buf, w_buf, a_high, a_low, b_high, b_low,
    g_buf, h_buf,
    left_sum, right_sum, left_send, right_send, left_recv, right_recv,
    local_sem, a_send_sem, a_recv_sem, b_send_sem, b_recv_sem,
    l_send_sem, l_recv_sem, r_send_sem, r_recv_sem,
):
    seqs, res, feats = a_hbm.shape
    feats_e = b_hbm.shape[2]
    tile_j = res
    tile_i = d_hbm.shape[0] // tile_j
    halves = tile_i // res
    total = seqs * rows
    group_c = WIDE // feats_e
    group_e = WIDE // feats
    chunks_c = feats // group_c
    chunks_e = feats_e // group_e

    r = lax.axis_index("row")
    q = lax.axis_index("col")
    owner_row = q // halves
    part = q % halves
    inside = owner_row == r

    copy_d = pltpu.make_async_copy(d_hbm, d_buf, local_sem.at[0])
    copy_w = pltpu.make_async_copy(w_hbm, w_buf, local_sem.at[1])
    fetch_a = pltpu.make_async_copy(a_hbm, a_own, local_sem.at[2])
    fetch_b = pltpu.make_async_copy(b_hbm, b_own, local_sem.at[3])
    fetch_b.start()
    fetch_a.start()
    copy_d.start()
    copy_w.start()

    barrier = pltpu.get_barrier_semaphore()

    def signal(row, col):
        pl.semaphore_signal(barrier, inc=1, device_id=(row, col), device_id_type=MESH)

    def arrived(ref, sem):
        pltpu.make_async_copy(ref, ref, sem).wait()

    def owners(act, own):
        for step in range(1, cols):
            act((q + step) % cols, 0)
        pl.when(jnp.logical_not(inside))(lambda: act(q, 1))
        if own is not None:
            pl.when(inside)(own)

    def sources(act, own):
        for step in range(1, rows):
            for h in range(halves):
                act((r + step) % rows, h, 0)
        for step in range(1, halves):
            act(r, (part + step) % halves, 0)
        pl.when(jnp.logical_not(inside))(lambda: act(r, part, 1))
        if own is not None:
            pl.when(inside)(own)

    sources(lambda row, h, _: signal(row, r * halves + h), None)
    for step in range(1, rows):
        signal((r + step) % rows, q)

    fetch_b.wait()
    b_pack[...] = jnp.concatenate([b_own[s] for s in range(seqs)], axis=1)
    fetch_a.wait()
    a_pack[...] = jnp.concatenate([a_own[s] for s in range(seqs)], axis=1)

    pl.semaphore_wait(barrier, (rows - 1) + jnp.where(inside, cols - 1, cols))

    def send_a(col, which):
        pltpu.make_async_remote_copy(
            src_ref=a_pack, dst_ref=a_all.at[part, r], send_sem=a_send_sem.at[which],
            recv_sem=a_recv_sem, device_id=(owner_row, col), device_id_type=MESH).start()

    owners(send_a, lambda: pltpu.make_async_copy(a_pack, a_all.at[part, r], a_recv_sem).start())

    for step in range(1, rows):
        pltpu.make_async_remote_copy(
            src_ref=b_pack, dst_ref=b_all.at[r], send_sem=b_send_sem, recv_sem=b_recv_sem,
            device_id=((r + step) % rows, q), device_id_type=MESH).start()
    pltpu.make_async_copy(b_pack, b_all.at[r], b_recv_sem).start()

    copy_d.wait()
    copy_w.wait()
    d_plain = d_buf[...]
    d_turned = jnp.concatenate(
        [d_buf[pl.ds(j, tile_i, stride=tile_j), :] for j in range(tile_j)], axis=0)

    def expand(d, w, chunks, place):
        d_high, d_low = split(d)
        d_all = jnp.concatenate([d_high, d_low, d_high], axis=1)
        for first in range(0, chunks, SPAN):
            group = range(first, min(first + SPAN, chunks))
            w_high, w_low = split(jnp.concatenate([w(n) for n in group], axis=0))
            out = dot_nt(d_all, jnp.concatenate([w_high, w_high, w_low], axis=1))
            for low, value in enumerate(split(out)):
                for n in group:
                    place(low, n, value[:, (n - first) * WIDE:(n - first + 1) * WIDE])

    def place_g(low, n, value):
        for j in range(tile_j):
            for h in range(halves):
                top = ((low * halves + h) * chunks_c + n) * res
                g_buf[top:top + res, j * WIDE:(j + 1) * WIDE] = value[
                    j * tile_i + h * res:j * tile_i + (h + 1) * res]

    def place_h(low, n, value):
        top = (low * chunks_e + n) * tile_j
        for i in range(tile_i):
            h_buf[top:top + tile_j, i * WIDE:(i + 1) * WIDE] = value[i * tile_j:(i + 1) * tile_j]

    expand(d_turned, lambda n: w_buf[n * WIDE:(n + 1) * WIDE, :], chunks_c, place_g)
    expand(d_plain, lambda n: jnp.concatenate(
        [w_buf[pl.ds(n * group_e + e, feats, stride=feats_e), :] for e in range(group_e)], axis=0),
        chunks_e, place_h)

    def repeat_lanes(x, width, high_ref, low_ref, base):
        size = x.shape[0]
        source = lax.broadcasted_iota(jnp.int32, (LANES, seqs * LANES), 0)
        target = lax.broadcasted_iota(jnp.int32, (LANES, seqs * LANES), 1)
        unit = (source == target // LANES * width + target % width).astype(jnp.bfloat16)
        for part_of, ref in zip(split(x), (high_ref, low_ref)):
            out = jnp.dot(part_of, unit, preferred_element_type=jnp.float32)
            for s in range(seqs):
                ref[base + s * size:base + (s + 1) * size, :] = out[:, s * LANES:(s + 1) * LANES]

    def masks(group, width):
        lane = lax.broadcasted_iota(jnp.int32, (group, WIDE), 1) // width
        block = lax.broadcasted_iota(jnp.int32, (group, WIDE), 0)
        return (lane == block).astype(jnp.float32).astype(jnp.bfloat16)

    def spread(ref, start, mask):
        x = ref[pl.ds(start, total, stride=res), :].astype(jnp.bfloat16)
        return jnp.concatenate([x * mask[k:k + 1] for k in range(mask.shape[0])], axis=0)

    def contract(count, coef, mat):
        acc = None
        for first in range(0, count, DEPTH):
            last = min(first + DEPTH, count)
            lhs = jnp.concatenate([coef(n) for n in range(first, last)], axis=1)
            term = dot_nt(lhs, mat[:, first * WIDE:last * WIDE])
            acc = term if acc is None else acc + term
        size, width = acc.shape[0] // 2, acc.shape[1] // 2
        return acc[:size, :width] + acc[:size, width:] + acc[size:, :width]

    def piece(ref, k, group):
        return jnp.concatenate(
            [ref[pl.ds(s * rows + k, group, stride=total), :] for s in range(seqs)], axis=0)

    arrived(b_all, b_recv_sem)
    repeat_lanes(b_all[...].reshape(rows * res, LANES), feats_e, b_high, b_low, 0)
    mask_c = masks(group_c, feats_e)

    def left_coef(j):
        return jnp.concatenate([spread(b_high, j, mask_c), spread(b_low, j, mask_c)], axis=0)

    left = contract(tile_j, left_coef, g_buf)
    for h in range(halves):
        left_sum[h] = left[:, h * LANES:(h + 1) * LANES]
    for k in range(rows):
        for h in range(halves):
            left_send[k, h] = piece(left_sum.at[h], k, group_c)

    def send_l(row, h, which):
        pltpu.make_async_remote_copy(
            src_ref=left_send.at[row, h], dst_ref=left_recv.at[q], send_sem=l_send_sem.at[which],
            recv_sem=l_recv_sem, device_id=(row, r * halves + h), device_id_type=MESH).start()

    arrived(a_all, a_recv_sem)
    sources(send_l, lambda: pltpu.make_async_copy(
        left_send.at[r, part], left_recv.at[q], l_recv_sem).start())

    for h in range(halves):
        repeat_lanes(a_all[h].reshape(rows * res, LANES), feats, a_high, a_low, h * total * res)
    mask_e = masks(group_e, feats)

    def right_coef(i):
        start = (i // res) * total * res + i % res
        return jnp.concatenate([spread(a_high, start, mask_e), spread(a_low, start, mask_e)], axis=0)

    right_sum[...] = contract(tile_i, right_coef, h_buf)
    for k in range(rows):
        right_send[k] = piece(right_sum, k, group_e)

    for step in range(1, rows):
        dest = (r + step) % rows
        pltpu.make_async_remote_copy(
            src_ref=right_send.at[dest], dst_ref=right_recv.at[r], send_sem=r_send_sem,
            recv_sem=r_recv_sem, device_id=(dest, q), device_id_type=MESH).start()
    pltpu.make_async_copy(right_send.at[r], right_recv.at[r], r_recv_sem).start()

    arrived(left_recv, l_recv_sem)
    size = left_recv.shape[1]
    out_ref[:size, :] = jnp.sum(left_recv[...], axis=0) / total
    arrived(right_recv, r_recv_sem)
    out_ref[size:, :] = jnp.sum(right_recv[...], axis=0) / total

    arrived(b_all.at[pl.ds(0, rows - 1)], b_send_sem)
    arrived(right_recv.at[pl.ds(0, rows - 1)], r_send_sem)
    arrived(left_recv.at[pl.ds(0, cols - 1)], l_send_sem.at[0])
    arrived(d_buf.at[pl.ds(0, (cols - 1) * res)], a_send_sem.at[0])

    @pl.when(jnp.logical_not(inside))
    def _():
        arrived(left_recv.at[0], l_send_sem.at[1])
        arrived(a_pack, a_send_sem.at[1])


def unfold(group_c, group_e, sums_ref, left_out, right_out):
    size = left_out.size // LANES
    for group, ref, out in (
        (group_c, sums_ref.at[:size], left_out), (group_e, sums_ref.at[size:], right_out)
    ):
        seqs, res, feats = out.shape
        x = ref[...].T
        each = ref.shape[0] // group
        chunks = feats // group
        for s in range(seqs):
            u, v = s // each, s % each
            out[s] = jnp.concatenate(
                [x[(u * chunks + n) * res:(u * chunks + n + 1) * res, v * group:(v + 1) * group]
                 for n in range(chunks)], axis=1)


def on_device(rows, cols, a, b, d, w):
    seqs, res, feats = a.shape
    feats_e = b.shape[2]
    tile_i, tile_j, pair = d.shape
    halves = tile_i // res
    total = seqs * rows
    group_c, group_e = WIDE // feats_e, WIDE // feats
    chunks_c, chunks_e = feats // group_c, feats_e // group_e
    pairs = tile_i * tile_j
    vmem = pl.BlockSpec(memory_space=pltpu.VMEM)
    hbm = pl.BlockSpec(memory_space=pltpu.HBM)
    f32, bf16 = jnp.float32, jnp.bfloat16
    left_piece = (seqs * feats * res // LANES, LANES)
    right_piece = (seqs * feats_e * res // LANES, LANES)
    dma = pltpu.SemaphoreType.DMA
    sums = pl.pallas_call(
        functools.partial(kernel, rows, cols),
        out_shape=jax.ShapeDtypeStruct((left_piece[0] + right_piece[0], LANES), f32),
        in_specs=[hbm] * 4,
        out_specs=vmem,
        scratch_shapes=[
            pltpu.VMEM(a.shape, f32),
            pltpu.VMEM(b.shape, f32),
            pltpu.VMEM((res, LANES), f32),
            pltpu.VMEM((res, LANES), f32),
            pltpu.VMEM((halves, rows, res, LANES), f32),
            pltpu.VMEM((rows, res, LANES), f32),
            pltpu.VMEM((pairs, pair), f32),
            pltpu.VMEM(w.shape, f32),
            pltpu.VMEM((total * tile_i, LANES), f32),
            pltpu.VMEM((total * tile_i, LANES), f32),
            pltpu.VMEM((total * tile_j, LANES), f32),
            pltpu.VMEM((total * tile_j, LANES), f32),
            pltpu.VMEM((2 * chunks_c * tile_i, tile_j * WIDE), bf16),
            pltpu.VMEM((2 * chunks_e * tile_j, tile_i * WIDE), bf16),
            pltpu.VMEM((halves, total * group_c, LANES), f32),
            pltpu.VMEM((total * group_e, LANES), f32),
            pltpu.VMEM((rows, halves) + left_piece, f32),
            pltpu.VMEM((rows,) + right_piece, f32),
            pltpu.VMEM((cols,) + left_piece, f32),
            pltpu.VMEM((rows,) + right_piece, f32),
            dma((4,)),
            dma((2,)),
            dma(()),
            dma(()),
            dma(()),
            dma((2,)),
            dma(()),
            dma(()),
            dma(()),
        ],
        compiler_params=pltpu.CompilerParams(
            collective_id=0, has_side_effects=True, vmem_limit_bytes=60 * 2**20),
    )(a, b, d.reshape(pairs, pair), w)
    return pl.pallas_call(
        functools.partial(unfold, group_c, group_e),
        out_shape=(jax.ShapeDtypeStruct(a.shape, f32), jax.ShapeDtypeStruct(b.shape, f32)),
        in_specs=[vmem],
        out_specs=(vmem, vmem),
    )(sums)


def solution(mesh):
    spec = P("row", "col", None)
    return jax.shard_map(
        functools.partial(on_device, mesh.shape["row"], mesh.shape["col"]),
        mesh=mesh,
        in_specs=(spec, spec, spec, P()),
        out_specs=(spec, spec),
        check_vma=False,
    )
```

```python
import functools

import jax
import jax.numpy as jnp
from jax import lax
from jax.experimental import pallas as pl
from jax.experimental.pallas import tpu as pltpu
from jax.sharding import PartitionSpec as P

MESH = pl.DeviceIdType.MESH
WIDE = 128
SPAN = 2
LANES = 128
DEPTH = 8


def split(x):
    high = x.astype(jnp.bfloat16)
    low = (x - high.astype(jnp.float32)).astype(jnp.bfloat16)
    return high, low


def dot_nt(x, y):
    return lax.dot_general(x, y, (((1,), (1,)), ((), ())), preferred_element_type=jnp.float32)


def kernel(
    rows, cols,
    a_hbm, b_hbm, d_hbm, w_hbm, out_ref,
    a_own, b_own, a_pack, b_pack, a_all, b_all, d_buf, w_buf, a_high, a_low, b_high, b_low,
    g_buf, h_buf, unit_a, unit_b,
    left_sum, right_sum, left_send, right_send, left_recv, right_recv,
    local_sem, a_send_sem, a_recv_sem, b_send_sem, b_recv_sem,
    l_send_sem, l_recv_sem, r_send_sem, r_recv_sem,
):
    seqs, res, feats = a_hbm.shape
    feats_e = b_hbm.shape[2]
    tile_j = res
    tile_i = d_hbm.shape[0] // tile_j
    halves = tile_i // res
    total = seqs * rows
    group_c = WIDE // feats_e
    group_e = WIDE // feats
    chunks_c = feats // group_c
    chunks_e = feats_e // group_e

    r = lax.axis_index("row")
    q = lax.axis_index("col")
    owner_row = q // halves
    part = q % halves
    inside = owner_row == r

    copy_d = pltpu.make_async_copy(d_hbm, d_buf, local_sem.at[0])
    copy_w = pltpu.make_async_copy(w_hbm, w_buf, local_sem.at[1])
    fetch_a = pltpu.make_async_copy(a_hbm, a_own, local_sem.at[2])
    fetch_b = pltpu.make_async_copy(b_hbm, b_own, local_sem.at[3])
    fetch_b.start()
    fetch_a.start()
    copy_d.start()
    copy_w.start()

    barrier = pltpu.get_barrier_semaphore()

    def signal(row, col):
        pl.semaphore_signal(barrier, inc=1, device_id=(row, col), device_id_type=MESH)

    def arrived(ref, sem):
        pltpu.make_async_copy(ref, ref, sem).wait()

    def owners(act, own):
        for step in range(1, cols):
            act((q + step) % cols, 0)
        pl.when(jnp.logical_not(inside))(lambda: act(q, 1))
        if own is not None:
            pl.when(inside)(own)

    def sources(act, own):
        for step in range(1, rows):
            for h in range(halves):
                act((r + step) % rows, h, 0)
        for step in range(1, halves):
            act(r, (part + step) % halves, 0)
        pl.when(jnp.logical_not(inside))(lambda: act(r, part, 1))
        if own is not None:
            pl.when(inside)(own)

    sources(lambda row, h, _: signal(row, r * halves + h), None)
    for step in range(1, rows):
        signal((r + step) % rows, q)

    fetch_b.wait()
    b_pack[...] = jnp.concatenate([b_own[s] for s in range(seqs)], axis=1)
    fetch_a.wait()
    a_pack[...] = jnp.concatenate([a_own[s] for s in range(seqs)], axis=1)

    pl.semaphore_wait(barrier, (rows - 1) + jnp.where(inside, cols - 1, cols))

    def send_a(col, which):
        pltpu.make_async_remote_copy(
            src_ref=a_pack, dst_ref=a_all.at[part, r], send_sem=a_send_sem.at[which],
            recv_sem=a_recv_sem, device_id=(owner_row, col), device_id_type=MESH).start()

    owners(send_a, lambda: pltpu.make_async_copy(a_pack, a_all.at[part, r], a_recv_sem).start())

    for step in range(1, rows):
        pltpu.make_async_remote_copy(
            src_ref=b_pack, dst_ref=b_all.at[r], send_sem=b_send_sem, recv_sem=b_recv_sem,
            device_id=((r + step) % rows, q), device_id_type=MESH).start()
    pltpu.make_async_copy(b_pack, b_all.at[r], b_recv_sem).start()

    for unit, width in ((unit_a, feats), (unit_b, feats_e)):
        lane = lax.broadcasted_iota(jnp.int32, (LANES, LANES), 1)
        offset = lax.broadcasted_iota(jnp.int32, (LANES, LANES), 0) - lax.rem(lane, width)
        for s in range(seqs):
            unit[:, s * LANES:(s + 1) * LANES] = (offset == s * width).astype(
                jnp.float32).astype(jnp.bfloat16)

    def masks(group, width):
        lane = lax.broadcasted_iota(jnp.int32, (group, WIDE), 1) // width
        block = lax.broadcasted_iota(jnp.int32, (group, WIDE), 0)
        return (lane == block).astype(jnp.float32).astype(jnp.bfloat16)

    mask_c = masks(group_c, feats_e)
    mask_e = masks(group_e, feats)

    copy_d.wait()
    copy_w.wait()
    d_plain = d_buf[...]
    d_turned = jnp.concatenate(
        [d_buf[pl.ds(j, tile_i, stride=tile_j), :] for j in range(tile_j)], axis=0)

    def expand(d, w, chunks, place):
        d_high, d_low = split(d)
        d_all = jnp.concatenate([d_high, d_low, d_high], axis=1)
        for first in range(0, chunks, SPAN):
            group = range(first, min(first + SPAN, chunks))
            w_high, w_low = split(jnp.concatenate([w(n) for n in group], axis=0))
            out = dot_nt(d_all, jnp.concatenate([w_high, w_high, w_low], axis=1))
            for low, value in enumerate(split(out)):
                for n in group:
                    place(low, n, value[:, (n - first) * WIDE:(n - first + 1) * WIDE])

    def place_g(low, n, value):
        for j in range(tile_j):
            for h in range(halves):
                top = ((low * halves + h) * chunks_c + n) * res
                g_buf[top:top + res, j * WIDE:(j + 1) * WIDE] = value[
                    j * tile_i + h * res:j * tile_i + (h + 1) * res]

    def place_h(low, n, value):
        top = (low * chunks_e + n) * tile_j
        for i in range(tile_i):
            h_buf[top:top + tile_j, i * WIDE:(i + 1) * WIDE] = value[i * tile_j:(i + 1) * tile_j]

    expand(d_turned, lambda n: w_buf[n * WIDE:(n + 1) * WIDE, :], chunks_c, place_g)
    expand(d_plain, lambda n: jnp.concatenate(
        [w_buf[pl.ds(n * group_e + e, feats, stride=feats_e), :] for e in range(group_e)], axis=0),
        chunks_e, place_h)

    def repeat_lanes(x, unit, parts, high_ref, low_ref):
        size = x.shape[0] // parts
        for part_of, ref in zip(split(x), (high_ref, low_ref)):
            out = jnp.dot(part_of, unit[...], preferred_element_type=jnp.float32)
            for h in range(parts):
                for s in range(seqs):
                    ref[(h * seqs + s) * size:(h * seqs + s + 1) * size, :] = out[
                        h * size:(h + 1) * size, s * LANES:(s + 1) * LANES]

    def spread(ref, start, mask):
        x = ref[pl.ds(start, total, stride=res), :].astype(jnp.bfloat16)
        return jnp.concatenate([x * mask[k:k + 1] for k in range(mask.shape[0])], axis=0)

    def contract(count, coef, mat):
        acc = None
        for first in range(0, count, DEPTH):
            last = min(first + DEPTH, count)
            lhs = jnp.concatenate([coef(n) for n in range(first, last)], axis=1)
            term = dot_nt(lhs, mat[:, first * WIDE:last * WIDE])
            acc = term if acc is None else acc + term
        size, width = acc.shape[0] // 2, acc.shape[1] // 2
        return acc[:size, :width] + acc[:size, width:] + acc[size:, :width]

    def piece(ref, k, group):
        return jnp.concatenate(
            [ref[pl.ds(s * rows + k, group, stride=total), :] for s in range(seqs)], axis=0)

    arrived(b_all, b_recv_sem)
    repeat_lanes(b_all[...].reshape(rows * res, LANES), unit_b, 1, b_high, b_low)

    def left_coef(j):
        return jnp.concatenate([spread(b_high, j, mask_c), spread(b_low, j, mask_c)], axis=0)

    left = contract(tile_j, left_coef, g_buf)
    for h in range(halves):
        left_sum[h] = left[:, h * LANES:(h + 1) * LANES]
    for k in range(rows):
        for h in range(halves):
            left_send[k, h] = piece(left_sum.at[h], k, group_c)

    def send_l(row, h, which):
        pltpu.make_async_remote_copy(
            src_ref=left_send.at[row, h], dst_ref=left_recv.at[q], send_sem=l_send_sem.at[which],
            recv_sem=l_recv_sem, device_id=(row, r * halves + h), device_id_type=MESH).start()

    arrived(a_all, a_recv_sem)
    sources(send_l, lambda: pltpu.make_async_copy(
        left_send.at[r, part], left_recv.at[q], l_recv_sem).start())

    repeat_lanes(a_all[...].reshape(halves * rows * res, LANES), unit_a, halves, a_high, a_low)

    def right_coef(i):
        start = (i // res) * total * res + i % res
        return jnp.concatenate([spread(a_high, start, mask_e), spread(a_low, start, mask_e)], axis=0)

    right_sum[...] = contract(tile_i, right_coef, h_buf)
    for k in range(rows):
        right_send[k] = piece(right_sum, k, group_e)

    for step in range(1, rows):
        dest = (r + step) % rows
        pltpu.make_async_remote_copy(
            src_ref=right_send.at[dest], dst_ref=right_recv.at[r], send_sem=r_send_sem,
            recv_sem=r_recv_sem, device_id=(dest, q), device_id_type=MESH).start()
    pltpu.make_async_copy(right_send.at[r], right_recv.at[r], r_recv_sem).start()

    arrived(left_recv, l_recv_sem)
    size = left_recv.shape[1]
    out_ref[:size, :] = jnp.sum(left_recv[...], axis=0) / total
    arrived(right_recv, r_recv_sem)
    out_ref[size:, :] = jnp.sum(right_recv[...], axis=0) / total

    arrived(b_all.at[pl.ds(0, rows - 1)], b_send_sem)
    arrived(right_recv.at[pl.ds(0, rows - 1)], r_send_sem)
    arrived(left_recv.at[pl.ds(0, cols - 1)], l_send_sem.at[0])
    arrived(d_buf.at[pl.ds(0, (cols - 1) * res)], a_send_sem.at[0])

    @pl.when(jnp.logical_not(inside))
    def _():
        arrived(left_recv.at[0], l_send_sem.at[1])
        arrived(a_pack, a_send_sem.at[1])


def unfold(group_c, group_e, sums_ref, left_out, right_out):
    size = left_out.size // LANES
    for group, ref, out in (
        (group_c, sums_ref.at[:size], left_out), (group_e, sums_ref.at[size:], right_out)
    ):
        seqs, res, feats = out.shape
        x = ref[...].T
        each = ref.shape[0] // group
        chunks = feats // group
        for s in range(seqs):
            u, v = s // each, s % each
            out[s] = jnp.concatenate(
                [x[(u * chunks + n) * res:(u * chunks + n + 1) * res, v * group:(v + 1) * group]
                 for n in range(chunks)], axis=1)


def on_device(rows, cols, a, b, d, w):
    seqs, res, feats = a.shape
    feats_e = b.shape[2]
    tile_i, tile_j, pair = d.shape
    halves = tile_i // res
    total = seqs * rows
    group_c, group_e = WIDE // feats_e, WIDE // feats
    chunks_c, chunks_e = feats // group_c, feats_e // group_e
    pairs = tile_i * tile_j
    vmem = pl.BlockSpec(memory_space=pltpu.VMEM)
    hbm = pl.BlockSpec(memory_space=pltpu.HBM)
    f32, bf16 = jnp.float32, jnp.bfloat16
    left_piece = (seqs * feats * res // LANES, LANES)
    right_piece = (seqs * feats_e * res // LANES, LANES)
    dma = pltpu.SemaphoreType.DMA
    sums = pl.pallas_call(
        functools.partial(kernel, rows, cols),
        out_shape=jax.ShapeDtypeStruct((left_piece[0] + right_piece[0], LANES), f32),
        in_specs=[hbm] * 4,
        out_specs=vmem,
        scratch_shapes=[
            pltpu.VMEM(a.shape, f32),
            pltpu.VMEM(b.shape, f32),
            pltpu.VMEM((res, LANES), f32),
            pltpu.VMEM((res, LANES), f32),
            pltpu.VMEM((halves, rows, res, LANES), f32),
            pltpu.VMEM((rows, res, LANES), f32),
            pltpu.VMEM((pairs, pair), f32),
            pltpu.VMEM(w.shape, f32),
            pltpu.VMEM((total * tile_i, LANES), f32),
            pltpu.VMEM((total * tile_i, LANES), f32),
            pltpu.VMEM((total * tile_j, LANES), f32),
            pltpu.VMEM((total * tile_j, LANES), f32),
            pltpu.VMEM((2 * chunks_c * tile_i, tile_j * WIDE), bf16),
            pltpu.VMEM((2 * chunks_e * tile_j, tile_i * WIDE), bf16),
            pltpu.VMEM((LANES, seqs * LANES), bf16),
            pltpu.VMEM((LANES, seqs * LANES), bf16),
            pltpu.VMEM((halves, total * group_c, LANES), f32),
            pltpu.VMEM((total * group_e, LANES), f32),
            pltpu.VMEM((rows, halves) + left_piece, f32),
            pltpu.VMEM((rows,) + right_piece, f32),
            pltpu.VMEM((cols,) + left_piece, f32),
            pltpu.VMEM((rows,) + right_piece, f32),
            dma((4,)),
            dma((2,)),
            dma(()),
            dma(()),
            dma(()),
            dma((2,)),
            dma(()),
            dma(()),
            dma(()),
        ],
        compiler_params=pltpu.CompilerParams(
            collective_id=0, has_side_effects=True, vmem_limit_bytes=60 * 2**20),
    )(a, b, d.reshape(pairs, pair), w)
    return pl.pallas_call(
        functools.partial(unfold, group_c, group_e),
        out_shape=(jax.ShapeDtypeStruct(a.shape, f32), jax.ShapeDtypeStruct(b.shape, f32)),
        in_specs=[vmem],
        out_specs=(vmem, vmem),
    )(sums)


def solution(mesh):
    spec = P("row", "col", None)
    return jax.shard_map(
        functools.partial(on_device, mesh.shape["row"], mesh.shape["col"]),
        mesh=mesh,
        in_specs=(spec, spec, spec, P()),
        out_specs=(spec, spec),
        check_vma=False,
    )
```

```python
import functools

import jax
import jax.numpy as jnp
from jax import lax
from jax.experimental import pallas as pl
from jax.experimental.pallas import tpu as pltpu
from jax.sharding import PartitionSpec as P

MESH = pl.DeviceIdType.MESH
WIDE = 128
SPAN = 2
LANES = 128
DEPTH = 8


def split(x):
    high = x.astype(jnp.bfloat16)
    low = (x - high.astype(jnp.float32)).astype(jnp.bfloat16)
    return high, low


def dot_nt(x, y):
    return lax.dot_general(x, y, (((1,), (1,)), ((), ())), preferred_element_type=jnp.float32)


def kernel(
    rows, cols,
    a_hbm, b_hbm, d_hbm, w_hbm, out_ref,
    a_own, b_own, a_pack, b_pack, a_all, b_all, d_buf, w_buf, a_high, a_low, b_high, b_low,
    g_buf, h_buf,
    left_sum, right_sum, left_send, right_send, left_recv, right_recv,
    local_sem, a_send_sem, a_recv_sem, b_send_sem, b_recv_sem,
    l_send_sem, l_recv_sem, r_send_sem, r_recv_sem,
):
    seqs, res, feats = a_hbm.shape
    feats_e = b_hbm.shape[2]
    tile_j = res
    tile_i = d_hbm.shape[0] // tile_j
    halves = tile_i // res
    total = seqs * rows
    group_c = WIDE // feats_e
    group_e = WIDE // feats
    chunks_c = feats // group_c
    chunks_e = feats_e // group_e

    r = lax.axis_index("row")
    q = lax.axis_index("col")
    owner_row = q // halves
    part = q % halves
    inside = owner_row == r

    copy_d = pltpu.make_async_copy(d_hbm, d_buf, local_sem.at[0])
    copy_w = pltpu.make_async_copy(w_hbm, w_buf, local_sem.at[1])
    fetch_a = pltpu.make_async_copy(a_hbm, a_own, local_sem.at[2])
    fetch_b = pltpu.make_async_copy(b_hbm, b_own, local_sem.at[3])
    fetch_b.start()
    fetch_a.start()
    copy_d.start()
    copy_w.start()

    barrier = pltpu.get_barrier_semaphore()

    def signal(row, col):
        pl.semaphore_signal(barrier, inc=1, device_id=(row, col), device_id_type=MESH)

    def arrived(ref, sem):
        pltpu.make_async_copy(ref, ref, sem).wait()

    def owners(act, own):
        for step in range(1, cols):
            act((q + step) % cols, 0)
        pl.when(jnp.logical_not(inside))(lambda: act(q, 1))
        if own is not None:
            pl.when(inside)(own)

    def sources(act, own):
        for step in range(1, rows):
            for h in range(halves):
                act((r + step) % rows, h, 0)
        for step in range(1, halves):
            act(r, (part + step) % halves, 0)
        pl.when(jnp.logical_not(inside))(lambda: act(r, part, 1))
        if own is not None:
            pl.when(inside)(own)

    owners(lambda col, _: signal(owner_row, col), None)
    sources(lambda row, h, _: signal(row, r * halves + h), None)
    for step in range(1, rows):
        signal((r + step) % rows, q)

    copy_d.wait()
    copy_w.wait()
    d_plain = d_buf[...]
    d_turned = jnp.concatenate(
        [d_buf[pl.ds(j, tile_i, stride=tile_j), :] for j in range(tile_j)], axis=0)

    def expand(d, w, chunks, place):
        d_high, d_low = split(d)
        d_all = jnp.concatenate([d_high, d_low, d_high], axis=1)
        for first in range(0, chunks, SPAN):
            group = range(first, min(first + SPAN, chunks))
            w_high, w_low = split(jnp.concatenate([w(n) for n in group], axis=0))
            out = dot_nt(d_all, jnp.concatenate([w_high, w_high, w_low], axis=1))
            for low, value in enumerate(split(out)):
                for n in group:
                    place(low, n, value[:, (n - first) * WIDE:(n - first + 1) * WIDE])

    def place_g(low, n, value):
        for j in range(tile_j):
            for h in range(halves):
                top = ((low * halves + h) * chunks_c + n) * res
                g_buf[top:top + res, j * WIDE:(j + 1) * WIDE] = value[
                    j * tile_i + h * res:j * tile_i + (h + 1) * res]

    def place_h(low, n, value):
        top = (low * chunks_e + n) * tile_j
        for i in range(tile_i):
            h_buf[top:top + tile_j, i * WIDE:(i + 1) * WIDE] = value[i * tile_j:(i + 1) * tile_j]

    expand(d_turned, lambda n: w_buf[n * WIDE:(n + 1) * WIDE, :], chunks_c, place_g)
    fetch_b.wait()
    b_pack[...] = jnp.concatenate([b_own[s] for s in range(seqs)], axis=1)
    fetch_a.wait()
    a_pack[...] = jnp.concatenate([a_own[s] for s in range(seqs)], axis=1)

    pl.semaphore_wait(barrier, (rows - 1) + 2 * jnp.where(inside, cols - 1, cols))

    for step in range(1, rows):
        pltpu.make_async_remote_copy(
            src_ref=b_pack, dst_ref=b_all.at[r], send_sem=b_send_sem, recv_sem=b_recv_sem,
            device_id=((r + step) % rows, q), device_id_type=MESH).start()
    pltpu.make_async_copy(b_pack, b_all.at[r], b_recv_sem).start()

    def send_a(col, which):
        pltpu.make_async_remote_copy(
            src_ref=a_pack, dst_ref=a_all.at[part, r], send_sem=a_send_sem.at[which],
            recv_sem=a_recv_sem, device_id=(owner_row, col), device_id_type=MESH).start()

    owners(send_a, lambda: pltpu.make_async_copy(a_pack, a_all.at[part, r], a_recv_sem).start())

    expand(d_plain, lambda n: jnp.concatenate(
        [w_buf[pl.ds(n * group_e + e, feats, stride=feats_e), :] for e in range(group_e)], axis=0),
        chunks_e, place_h)

    def repeat_lanes(x, width, high_ref, low_ref, base):
        size = x.shape[0]
        source = lax.broadcasted_iota(jnp.int32, (LANES, seqs * LANES), 0)
        target = lax.broadcasted_iota(jnp.int32, (LANES, seqs * LANES), 1)
        unit = (source == target // LANES * width + target % width).astype(jnp.bfloat16)
        for part_of, ref in zip(split(x), (high_ref, low_ref)):
            out = jnp.dot(part_of, unit, preferred_element_type=jnp.float32)
            for s in range(seqs):
                ref[base + s * size:base + (s + 1) * size, :] = out[:, s * LANES:(s + 1) * LANES]

    def masks(group, width):
        lane = lax.broadcasted_iota(jnp.int32, (group, WIDE), 1) // width
        block = lax.broadcasted_iota(jnp.int32, (group, WIDE), 0)
        return (lane == block).astype(jnp.float32).astype(jnp.bfloat16)

    def spread(ref, start, mask):
        x = ref[pl.ds(start, total, stride=res), :].astype(jnp.bfloat16)
        return jnp.concatenate([x * mask[k:k + 1] for k in range(mask.shape[0])], axis=0)

    def contract(count, coef, mat):
        acc = None
        for first in range(0, count, DEPTH):
            last = min(first + DEPTH, count)
            lhs = jnp.concatenate([coef(n) for n in range(first, last)], axis=1)
            term = dot_nt(lhs, mat[:, first * WIDE:last * WIDE])
            acc = term if acc is None else acc + term
        size, width = acc.shape[0] // 2, acc.shape[1] // 2
        return acc[:size, :width] + acc[:size, width:] + acc[size:, :width]

    def piece(ref, k, group):
        return jnp.concatenate(
            [ref[pl.ds(s * rows + k, group, stride=total), :] for s in range(seqs)], axis=0)

    arrived(b_all, b_recv_sem)
    repeat_lanes(b_all[...].reshape(rows * res, LANES), feats_e, b_high, b_low, 0)
    mask_c = masks(group_c, feats_e)

    def left_coef(j):
        return jnp.concatenate([spread(b_high, j, mask_c), spread(b_low, j, mask_c)], axis=0)

    left = contract(tile_j, left_coef, g_buf)
    for h in range(halves):
        left_sum[h] = left[:, h * LANES:(h + 1) * LANES]
    for k in range(rows):
        for h in range(halves):
            left_send[k, h] = piece(left_sum.at[h], k, group_c)

    def send_l(row, h, which):
        pltpu.make_async_remote_copy(
            src_ref=left_send.at[row, h], dst_ref=left_recv.at[q], send_sem=l_send_sem.at[which],
            recv_sem=l_recv_sem, device_id=(row, r * halves + h), device_id_type=MESH).start()

    sources(send_l, lambda: pltpu.make_async_copy(
        left_send.at[r, part], left_recv.at[q], l_recv_sem).start())

    arrived(a_all, a_recv_sem)
    for h in range(halves):
        repeat_lanes(a_all[h].reshape(rows * res, LANES), feats, a_high, a_low, h * total * res)
    mask_e = masks(group_e, feats)

    def right_coef(i):
        start = (i // res) * total * res + i % res
        return jnp.concatenate([spread(a_high, start, mask_e), spread(a_low, start, mask_e)], axis=0)

    right_sum[...] = contract(tile_i, right_coef, h_buf)
    for k in range(rows):
        right_send[k] = piece(right_sum, k, group_e)

    for step in range(1, rows):
        dest = (r + step) % rows
        pltpu.make_async_remote_copy(
            src_ref=right_send.at[dest], dst_ref=right_recv.at[r], send_sem=r_send_sem,
            recv_sem=r_recv_sem, device_id=(dest, q), device_id_type=MESH).start()
    pltpu.make_async_copy(right_send.at[r], right_recv.at[r], r_recv_sem).start()

    arrived(left_recv, l_recv_sem)
    size = left_recv.shape[1]
    out_ref[:size, :] = jnp.sum(left_recv[...], axis=0) / total
    arrived(right_recv, r_recv_sem)
    out_ref[size:, :] = jnp.sum(right_recv[...], axis=0) / total

    arrived(b_all.at[pl.ds(0, rows - 1)], b_send_sem)
    arrived(right_recv.at[pl.ds(0, rows - 1)], r_send_sem)
    arrived(left_recv.at[pl.ds(0, cols - 1)], l_send_sem.at[0])
    arrived(d_buf.at[pl.ds(0, (cols - 1) * res)], a_send_sem.at[0])

    @pl.when(jnp.logical_not(inside))
    def _():
        arrived(left_recv.at[0], l_send_sem.at[1])
        arrived(a_pack, a_send_sem.at[1])


def unfold(group_c, group_e, sums_ref, left_out, right_out):
    size = left_out.size // LANES
    for group, ref, out in (
        (group_c, sums_ref.at[:size], left_out), (group_e, sums_ref.at[size:], right_out)
    ):
        seqs, res, feats = out.shape
        x = ref[...].T
        each = ref.shape[0] // group
        chunks = feats // group
        for s in range(seqs):
            u, v = s // each, s % each
            out[s] = jnp.concatenate(
                [x[(u * chunks + n) * res:(u * chunks + n + 1) * res, v * group:(v + 1) * group]
                 for n in range(chunks)], axis=1)


def on_device(rows, cols, a, b, d, w):
    seqs, res, feats = a.shape
    feats_e = b.shape[2]
    tile_i, tile_j, pair = d.shape
    halves = tile_i // res
    total = seqs * rows
    group_c, group_e = WIDE // feats_e, WIDE // feats
    chunks_c, chunks_e = feats // group_c, feats_e // group_e
    pairs = tile_i * tile_j
    vmem = pl.BlockSpec(memory_space=pltpu.VMEM)
    hbm = pl.BlockSpec(memory_space=pltpu.HBM)
    f32, bf16 = jnp.float32, jnp.bfloat16
    left_piece = (seqs * feats * res // LANES, LANES)
    right_piece = (seqs * feats_e * res // LANES, LANES)
    dma = pltpu.SemaphoreType.DMA
    sums = pl.pallas_call(
        functools.partial(kernel, rows, cols),
        out_shape=jax.ShapeDtypeStruct((left_piece[0] + right_piece[0], LANES), f32),
        in_specs=[hbm] * 4,
        out_specs=vmem,
        scratch_shapes=[
            pltpu.VMEM(a.shape, f32),
            pltpu.VMEM(b.shape, f32),
            pltpu.VMEM((res, LANES), f32),
            pltpu.VMEM((res, LANES), f32),
            pltpu.VMEM((halves, rows, res, LANES), f32),
            pltpu.VMEM((rows, res, LANES), f32),
            pltpu.VMEM((pairs, pair), f32),
            pltpu.VMEM(w.shape, f32),
            pltpu.VMEM((total * tile_i, LANES), f32),
            pltpu.VMEM((total * tile_i, LANES), f32),
            pltpu.VMEM((total * tile_j, LANES), f32),
            pltpu.VMEM((total * tile_j, LANES), f32),
            pltpu.VMEM((2 * chunks_c * tile_i, tile_j * WIDE), bf16),
            pltpu.VMEM((2 * chunks_e * tile_j, tile_i * WIDE), bf16),
            pltpu.VMEM((halves, total * group_c, LANES), f32),
            pltpu.VMEM((total * group_e, LANES), f32),
            pltpu.VMEM((rows, halves) + left_piece, f32),
            pltpu.VMEM((rows,) + right_piece, f32),
            pltpu.VMEM((cols,) + left_piece, f32),
            pltpu.VMEM((rows,) + right_piece, f32),
            dma((4,)),
            dma((2,)),
            dma(()),
            dma(()),
            dma(()),
            dma((2,)),
            dma(()),
            dma(()),
            dma(()),
        ],
        compiler_params=pltpu.CompilerParams(
            collective_id=0, has_side_effects=True, vmem_limit_bytes=60 * 2**20),
    )(a, b, d.reshape(pairs, pair), w)
    return pl.pallas_call(
        functools.partial(unfold, group_c, group_e),
        out_shape=(jax.ShapeDtypeStruct(a.shape, f32), jax.ShapeDtypeStruct(b.shape, f32)),
        in_specs=[vmem],
        out_specs=(vmem, vmem),
    )(sums)


def solution(mesh):
    spec = P("row", "col", None)
    return jax.shard_map(
        functools.partial(on_device, mesh.shape["row"], mesh.shape["col"]),
        mesh=mesh,
        in_specs=(spec, spec, spec, P()),
        out_specs=(spec, spec),
        check_vma=False,
    )
```

```python
import functools

import jax
import jax.numpy as jnp
from jax import lax
from jax.experimental import pallas as pl
from jax.experimental.pallas import tpu as pltpu
from jax.sharding import PartitionSpec as P

MESH = pl.DeviceIdType.MESH
WIDE = 128
SPAN = 2
LANES = 128
DEPTH = 8


def split(x):
    high = x.astype(jnp.bfloat16)
    low = (x - high.astype(jnp.float32)).astype(jnp.bfloat16)
    return high, low


def dot_nt(x, y):
    return lax.dot_general(x, y, (((1,), (1,)), ((), ())), preferred_element_type=jnp.float32)


def kernel(
    rows, cols,
    a_hbm, b_hbm, d_hbm, w_hbm, out_ref,
    a_own, b_own, a_pack, b_pack, a_all, b_all, d_buf, w_buf, a_high, a_low, b_high, b_low,
    g_buf, h_buf,
    left_sum, right_sum, left_send, right_send, left_recv, right_recv,
    local_sem, a_send_sem, a_recv_sem, b_send_sem, b_recv_sem,
    l_send_sem, l_recv_sem, r_send_sem, r_recv_sem,
):
    seqs, res, feats = a_hbm.shape
    feats_e = b_hbm.shape[2]
    tile_j = res
    tile_i = d_hbm.shape[0] // tile_j
    halves = tile_i // res
    total = seqs * rows
    group_c = WIDE // feats_e
    group_e = WIDE // feats
    chunks_c = feats // group_c
    chunks_e = feats_e // group_e

    r = lax.axis_index("row")
    q = lax.axis_index("col")
    owner_row = q // halves
    part = q % halves
    inside = owner_row == r

    copy_d = pltpu.make_async_copy(d_hbm, d_buf, local_sem.at[0])
    copy_w = pltpu.make_async_copy(w_hbm, w_buf, local_sem.at[1])
    fetch_a = pltpu.make_async_copy(a_hbm, a_own, local_sem.at[2])
    fetch_b = pltpu.make_async_copy(b_hbm, b_own, local_sem.at[3])
    fetch_b.start()
    fetch_a.start()
    copy_d.start()
    copy_w.start()

    barrier = pltpu.get_barrier_semaphore()

    def signal(row, col):
        pl.semaphore_signal(barrier, inc=1, device_id=(row, col), device_id_type=MESH)

    def arrived(ref, sem):
        pltpu.make_async_copy(ref, ref, sem).wait()

    def owners(act, own):
        for step in range(1, cols):
            act((q + step) % cols, 0)
        pl.when(jnp.logical_not(inside))(lambda: act(q, 1))
        if own is not None:
            pl.when(inside)(own)

    def sources(act, own):
        for step in range(1, rows):
            for h in range(halves):
                act((r + step) % rows, h, 0)
        for step in range(1, halves):
            act(r, (part + step) % halves, 0)
        pl.when(jnp.logical_not(inside))(lambda: act(r, part, 1))
        if own is not None:
            pl.when(inside)(own)

    owners(lambda col, _: signal(owner_row, col), None)
    sources(lambda row, h, _: signal(row, r * halves + h), None)
    for step in range(1, rows):
        signal((r + step) % rows, q)

    fetch_b.wait()
    b_pack[...] = jnp.concatenate([b_own[s] for s in range(seqs)], axis=1)
    fetch_a.wait()
    a_pack[...] = jnp.concatenate([a_own[s] for s in range(seqs)], axis=1)

    pl.semaphore_wait(barrier, (rows - 1) + 2 * jnp.where(inside, cols - 1, cols))

    for step in range(1, rows):
        pltpu.make_async_remote_copy(
            src_ref=b_pack, dst_ref=b_all.at[r], send_sem=b_send_sem, recv_sem=b_recv_sem,
            device_id=((r + step) % rows, q), device_id_type=MESH).start()
    pltpu.make_async_copy(b_pack, b_all.at[r], b_recv_sem).start()

    def send_a(col, which):
        pltpu.make_async_remote_copy(
            src_ref=a_pack, dst_ref=a_all.at[part, r], send_sem=a_send_sem.at[which],
            recv_sem=a_recv_sem, device_id=(owner_row, col), device_id_type=MESH).start()

    owners(send_a, lambda: pltpu.make_async_copy(a_pack, a_all.at[part, r], a_recv_sem).start())

    copy_d.wait()
    copy_w.wait()
    d_plain = d_buf[...]
    d_turned = jnp.concatenate(
        [d_buf[pl.ds(j, tile_i, stride=tile_j), :] for j in range(tile_j)], axis=0)

    def expand(d, w, chunks, place):
        d_high, d_low = split(d)
        d_all = jnp.concatenate([d_high, d_low, d_high], axis=1)
        for first in range(0, chunks, SPAN):
            group = range(first, min(first + SPAN, chunks))
            w_high, w_low = split(jnp.concatenate([w(n) for n in group], axis=0))
            out = dot_nt(d_all, jnp.concatenate([w_high, w_high, w_low], axis=1))
            for low, value in enumerate(split(out)):
                for n in group:
                    place(low, n, value[:, (n - first) * WIDE:(n - first + 1) * WIDE])

    def place_g(low, n, value):
        for j in range(tile_j):
            for h in range(halves):
                top = ((low * halves + h) * chunks_c + n) * res
                g_buf[top:top + res, j * WIDE:(j + 1) * WIDE] = value[
                    j * tile_i + h * res:j * tile_i + (h + 1) * res]

    def place_h(low, n, value):
        top = (low * chunks_e + n) * tile_j
        for i in range(tile_i):
            h_buf[top:top + tile_j, i * WIDE:(i + 1) * WIDE] = value[i * tile_j:(i + 1) * tile_j]

    expand(d_turned, lambda n: w_buf[n * WIDE:(n + 1) * WIDE, :], chunks_c, place_g)

    def repeat_lanes(x, width, high_ref, low_ref, base):
        size = x.shape[0]
        source = lax.broadcasted_iota(jnp.int32, (LANES, seqs * LANES), 0)
        target = lax.broadcasted_iota(jnp.int32, (LANES, seqs * LANES), 1)
        unit = (source == target // LANES * width + target % width).astype(jnp.bfloat16)
        for part_of, ref in zip(split(x), (high_ref, low_ref)):
            out = jnp.dot(part_of, unit, preferred_element_type=jnp.float32)
            for s in range(seqs):
                ref[base + s * size:base + (s + 1) * size, :] = out[:, s * LANES:(s + 1) * LANES]

    def masks(group, width):
        lane = lax.broadcasted_iota(jnp.int32, (group, WIDE), 1) // width
        block = lax.broadcasted_iota(jnp.int32, (group, WIDE), 0)
        return (lane == block).astype(jnp.float32).astype(jnp.bfloat16)

    def spread(ref, start, mask):
        x = ref[pl.ds(start, total, stride=res), :].astype(jnp.bfloat16)
        return jnp.concatenate([x * mask[k:k + 1] for k in range(mask.shape[0])], axis=0)

    def contract(count, coef, mat):
        acc = None
        for first in range(0, count, DEPTH):
            last = min(first + DEPTH, count)
            lhs = jnp.concatenate([coef(n) for n in range(first, last)], axis=1)
            term = dot_nt(lhs, mat[:, first * WIDE:last * WIDE])
            acc = term if acc is None else acc + term
        size, width = acc.shape[0] // 2, acc.shape[1] // 2
        return acc[:size, :width] + acc[:size, width:] + acc[size:, :width]

    def piece(ref, k, group):
        return jnp.concatenate(
            [ref[pl.ds(s * rows + k, group, stride=total), :] for s in range(seqs)], axis=0)

    arrived(b_all, b_recv_sem)
    repeat_lanes(b_all[...].reshape(rows * res, LANES), feats_e, b_high, b_low, 0)
    mask_c = masks(group_c, feats_e)

    def left_coef(j):
        return jnp.concatenate([spread(b_high, j, mask_c), spread(b_low, j, mask_c)], axis=0)

    left = contract(tile_j, left_coef, g_buf)
    for h in range(halves):
        left_sum[h] = left[:, h * LANES:(h + 1) * LANES]
    for k in range(rows):
        for h in range(halves):
            left_send[k, h] = piece(left_sum.at[h], k, group_c)

    def send_l(row, h, which):
        pltpu.make_async_remote_copy(
            src_ref=left_send.at[row, h], dst_ref=left_recv.at[q], send_sem=l_send_sem.at[which],
            recv_sem=l_recv_sem, device_id=(row, r * halves + h), device_id_type=MESH).start()

    sources(send_l, lambda: pltpu.make_async_copy(
        left_send.at[r, part], left_recv.at[q], l_recv_sem).start())

    expand(d_plain, lambda n: jnp.concatenate(
        [w_buf[pl.ds(n * group_e + e, feats, stride=feats_e), :] for e in range(group_e)], axis=0),
        chunks_e, place_h)
    arrived(a_all, a_recv_sem)
    for h in range(halves):
        repeat_lanes(a_all[h].reshape(rows * res, LANES), feats, a_high, a_low, h * total * res)
    mask_e = masks(group_e, feats)

    def right_coef(i):
        start = (i // res) * total * res + i % res
        return jnp.concatenate([spread(a_high, start, mask_e), spread(a_low, start, mask_e)], axis=0)

    right_sum[...] = contract(tile_i, right_coef, h_buf)
    for k in range(rows):
        right_send[k] = piece(right_sum, k, group_e)

    for step in range(1, rows):
        dest = (r + step) % rows
        pltpu.make_async_remote_copy(
            src_ref=right_send.at[dest], dst_ref=right_recv.at[r], send_sem=r_send_sem,
            recv_sem=r_recv_sem, device_id=(dest, q), device_id_type=MESH).start()
    pltpu.make_async_copy(right_send.at[r], right_recv.at[r], r_recv_sem).start()

    arrived(left_recv, l_recv_sem)
    size = left_recv.shape[1]
    out_ref[:size, :] = jnp.sum(left_recv[...], axis=0) / total
    arrived(right_recv, r_recv_sem)
    out_ref[size:, :] = jnp.sum(right_recv[...], axis=0) / total

    arrived(b_all.at[pl.ds(0, rows - 1)], b_send_sem)
    arrived(right_recv.at[pl.ds(0, rows - 1)], r_send_sem)
    arrived(left_recv.at[pl.ds(0, cols - 1)], l_send_sem.at[0])
    arrived(d_buf.at[pl.ds(0, (cols - 1) * res)], a_send_sem.at[0])

    @pl.when(jnp.logical_not(inside))
    def _():
        arrived(left_recv.at[0], l_send_sem.at[1])
        arrived(a_pack, a_send_sem.at[1])


def unfold(group_c, group_e, sums_ref, left_out, right_out):
    size = left_out.size // LANES
    for group, ref, out in (
        (group_c, sums_ref.at[:size], left_out), (group_e, sums_ref.at[size:], right_out)
    ):
        seqs, res, feats = out.shape
        x = ref[...].T
        each = ref.shape[0] // group
        chunks = feats // group
        for s in range(seqs):
            u, v = s // each, s % each
            out[s] = jnp.concatenate(
                [x[(u * chunks + n) * res:(u * chunks + n + 1) * res, v * group:(v + 1) * group]
                 for n in range(chunks)], axis=1)


def on_device(rows, cols, a, b, d, w):
    seqs, res, feats = a.shape
    feats_e = b.shape[2]
    tile_i, tile_j, pair = d.shape
    halves = tile_i // res
    total = seqs * rows
    group_c, group_e = WIDE // feats_e, WIDE // feats
    chunks_c, chunks_e = feats // group_c, feats_e // group_e
    pairs = tile_i * tile_j
    vmem = pl.BlockSpec(memory_space=pltpu.VMEM)
    hbm = pl.BlockSpec(memory_space=pltpu.HBM)
    f32, bf16 = jnp.float32, jnp.bfloat16
    left_piece = (seqs * feats * res // LANES, LANES)
    right_piece = (seqs * feats_e * res // LANES, LANES)
    dma = pltpu.SemaphoreType.DMA
    sums = pl.pallas_call(
        functools.partial(kernel, rows, cols),
        out_shape=jax.ShapeDtypeStruct((left_piece[0] + right_piece[0], LANES), f32),
        in_specs=[hbm] * 4,
        out_specs=vmem,
        scratch_shapes=[
            pltpu.VMEM(a.shape, f32),
            pltpu.VMEM(b.shape, f32),
            pltpu.VMEM((res, LANES), f32),
            pltpu.VMEM((res, LANES), f32),
            pltpu.VMEM((halves, rows, res, LANES), f32),
            pltpu.VMEM((rows, res, LANES), f32),
            pltpu.VMEM((pairs, pair), f32),
            pltpu.VMEM(w.shape, f32),
            pltpu.VMEM((total * tile_i, LANES), f32),
            pltpu.VMEM((total * tile_i, LANES), f32),
            pltpu.VMEM((total * tile_j, LANES), f32),
            pltpu.VMEM((total * tile_j, LANES), f32),
            pltpu.VMEM((2 * chunks_c * tile_i, tile_j * WIDE), bf16),
            pltpu.VMEM((2 * chunks_e * tile_j, tile_i * WIDE), bf16),
            pltpu.VMEM((halves, total * group_c, LANES), f32),
            pltpu.VMEM((total * group_e, LANES), f32),
            pltpu.VMEM((rows, halves) + left_piece, f32),
            pltpu.VMEM((rows,) + right_piece, f32),
            pltpu.VMEM((cols,) + left_piece, f32),
            pltpu.VMEM((rows,) + right_piece, f32),
            dma((4,)),
            dma((2,)),
            dma(()),
            dma(()),
            dma(()),
            dma((2,)),
            dma(()),
            dma(()),
            dma(()),
        ],
        compiler_params=pltpu.CompilerParams(
            collective_id=0, has_side_effects=True, vmem_limit_bytes=60 * 2**20),
    )(a, b, d.reshape(pairs, pair), w)
    return pl.pallas_call(
        functools.partial(unfold, group_c, group_e),
        out_shape=(jax.ShapeDtypeStruct(a.shape, f32), jax.ShapeDtypeStruct(b.shape, f32)),
        in_specs=[vmem],
        out_specs=(vmem, vmem),
    )(sums)


def solution(mesh):
    spec = P("row", "col", None)
    return jax.shard_map(
        functools.partial(on_device, mesh.shape["row"], mesh.shape["col"]),
        mesh=mesh,
        in_specs=(spec, spec, spec, P()),
        out_specs=(spec, spec),
        check_vma=False,
    )
```
